256 devices in a mesh: ka: 16 (over x_lo, y, core), kp: 8 (over z), ga: 2 (over x_hi).
Axes of the slice: x: 4 (x_hi: 2, x_lo: 2; x = x_hi * 2 + x_lo), y: 4, z: 8, core: 2. Of those that a mesh axis runs over, the one named last changes fastest.
Arguments:
- occupied: bfloat16 [16, 32, 64, 128], P('ka', 'kp', 'ga'), may hold values from -6 to 6
- virtual: bfloat16 [16, 256, 64, 128], P('ka', 'kp', 'ga'), may hold values from -6 to 6
- coulomb: float32 [16, 64, 64], P('ka'), may hold values from 0.3 to 3
- transfer_pairs: int32 [16, 2], P('ka'), may hold values from 0 to 15
- shifts: int32 [16, 2], P('ka'), may hold values from -1 to 1
Outputs:
- vertex: bfloat16 [16, 32, 256, 64, 128], P('ka', 'ga', None, 'kp')
The draws below stay inside these ranges and needn't reach their ends.
Inputs may be any that keep to these rules, and one draw needn't show every extreme that they name: `transfer_pairs`: row q names the first and the second k-point of the pair whose vertex is computed for momentum transfer q.
All inputs are finite; a program needn't handle non-finite values.
Results may differ from the reference program's by a relative error of at most 0.0064.
Values may be sent and summed in bfloat16 or wider, within the bound.
No kernel may reach another device: no remote copies, remote signals or barrier semaphores. Data moves between devices by JAX's collectives and lax.ppermute only.
A program may use at most 128 MiB of HBM per device.

```python
import math
import jax
import jax.numpy as jnp
from jax import lax

GRID = 64
NOCC = 32
NVIR = 256
NKPT = 16


def with_ends(result, stream_key, least, largest):
    extent = result.shape
    spot = [jax.random.randint(jax.random.fold_in(stream_key, axis), (), 0, extent[axis]) for axis in range(len(extent))]
    result = result.at[tuple(spot)].set(least)
    longest = extent.index(max(extent))
    spot[longest] = (spot[longest] + 1) % extent[longest]
    return result.at[tuple(spot)].set(largest)


def block_scale(key, shape, split, low, largest):
    factor_of = 1.0
    for dim, parts in split:
        draws = jax.random.uniform(jax.random.fold_in(jax.random.fold_in(key, 6), dim), (parts,), jnp.float32, low / len(split), largest / len(split))
        factor_of = factor_of * jnp.repeat(jnp.exp(draws), shape[dim] // parts).reshape((-1,) + (1,) * (len(shape) - 1 - dim))
    return factor_of


def bell_draw(key, shape, width, bound, split=(), kind=jnp.bfloat16):
    factor_of = block_scale(key, shape, split, -0.22, 0.18) if split else 1.0
    drawn = jax.random.normal(key, shape, jnp.float32) * width * factor_of
    return jnp.minimum(jnp.maximum(drawn, -bound), bound).astype(kind)


def setup_inputs(seed: int = 0) -> dict:
    key_of = jax.random.split(jax.random.key(seed), 6)
    occupied = bell_draw(key_of[0], (NKPT, NOCC, GRID, 2 * GRID), 1.0, 6.0, ((0, 16), (1, 8), (2, 2)))
    virtual = bell_draw(key_of[1], (NKPT, NVIR, GRID, 2 * GRID), 1.0, 6.0, ((0, 16), (1, 8), (2, 2)))
    coulomb = jnp.clip(jnp.exp(math.log(3.0) - 2.3025851 * jax.random.uniform(key_of[2], (NKPT, GRID, GRID), jnp.float32) ** block_scale(key_of[2], (NKPT, GRID, GRID), ((0, 16),), -0.2, 0.2)), 0.3, 3.0)
    transfer_pairs = with_ends(jax.random.randint(key_of[3], (NKPT, 2), 0, NKPT), jax.random.fold_in(key_of[3], 1), 0, NKPT - 1).astype(jnp.int32)
    shifts = with_ends(jax.random.randint(key_of[4], (NKPT, 2), -1, 2), jax.random.fold_in(key_of[4], 1), -1, 1).astype(jnp.int32)
    return dict(occupied=occupied, virtual=virtual, coulomb=coulomb, transfer_pairs=transfer_pairs, shifts=shifts)


def phase_angle_parts(points):
    index = jnp.arange(points, dtype=jnp.int32)
    windings = (index[:, None] * index[None, :]) % points
    angles = windings.astype(jnp.float32) * (2.0 * math.pi / points)
    return jnp.cos(angles), jnp.sin(angles)


def row_table_of(points):
    cosine, sine_part = phase_angle_parts(points)
    upper_rows = jnp.concatenate([cosine, -sine_part], 1)
    lower_rows = jnp.concatenate([sine_part, cosine], 1)
    return jnp.concatenate([upper_rows, lower_rows], 0).astype(jnp.bfloat16)


def col_table_of(points):
    cosine, sine_part = phase_angle_parts(points)
    return jnp.concatenate([cosine, sine_part], 0).astype(jnp.bfloat16)


def phase_grid(shift_pair, first_row, rows, points):
    xpos = first_row + jnp.arange(rows, dtype=jnp.int32)
    ypos = jnp.arange(points, dtype=jnp.int32)
    windings = (shift_pair[0] * xpos[:, None] + shift_pair[1] * ypos[None, :]) % points
    angles = windings.astype(jnp.float32) * (2.0 * math.pi / points)
    return jnp.cos(angles), -jnp.sin(angles)


def pair_spectra(occ_row, vir_rows, cosine, sine_part, row_table):
    points = row_table.shape[0] // 2
    occupied_values = occ_row.astype(jnp.float32)
    vir_values = vir_rows.astype(jnp.float32)
    occ_real, occ_imag = occupied_values[:, :points], occupied_values[:, points:]
    virtual_real, vir_imag = vir_values[..., :points], vir_values[..., points:]
    prod_real = occ_real * virtual_real + occ_imag * vir_imag
    prod_imag = occ_real * vir_imag - occ_imag * virtual_real
    rot_real = prod_real * cosine - prod_imag * sine_part
    rot_imag = prod_real * sine_part + prod_imag * cosine
    pair_field = jnp.concatenate([rot_real, rot_imag], -1).astype(jnp.bfloat16)
    fourier_spectra = jnp.einsum("vxk,kl->vxl", pair_field.astype(jnp.float32), row_table.astype(jnp.float32), precision=lax.Precision.HIGHEST)
    return fourier_spectra.astype(jnp.bfloat16)


def spectrum_x(fourier_spectra, kernel_q, column_lookup):
    points = column_lookup.shape[1]
    stacked_result = jnp.einsum("ja,dae->dje", column_lookup.astype(jnp.float32), fourier_spectra.astype(jnp.float32), precision=lax.Precision.HIGHEST)
    cos_part, sin_part = stacked_result[:, :points], stacked_result[:, points:]
    real_part = cos_part[..., :points] + sin_part[..., points:]
    imag_part = cos_part[..., points:] - sin_part[..., :points]
    scale = jnp.concatenate([kernel_q, kernel_q], -1) * (1.0 / points)
    return (jnp.concatenate([real_part, imag_part], -1) * scale).astype(jnp.bfloat16)


def reference(occupied, virtual, coulomb, transfer_pairs, shifts):
    points = occupied.shape[2]
    row_table = row_table_of(points)
    column_lookup = col_table_of(points)

    def one_transfer(packed):
        pair_row, shift_pair, kernel_q = packed
        occupied_q = lax.dynamic_index_in_dim(occupied, pair_row[0].astype(jnp.int32), 0, keepdims=False)
        virtual_q = lax.dynamic_index_in_dim(virtual, pair_row[1].astype(jnp.int32), 0, keepdims=False)
        cosine, sine_part = phase_grid(shift_pair, jnp.int32(0), points, points)

        def one_row(occ_row):
            return spectrum_x(pair_spectra(occ_row, virtual_q, cosine, sine_part, row_table), kernel_q, column_lookup)

        return lax.map(one_row, occupied_q)

    return lax.map(one_transfer, (transfer_pairs, shifts, coulomb))
```

```python
import math

import jax
import jax.numpy as jnp
import numpy as np
from jax import lax
from jax.experimental import pallas as pl
from jax.experimental.pallas import tpu as pltpu
from jax.sharding import PartitionSpec as P

F32 = jnp.float32
BF16 = jnp.bfloat16
VMEM = pltpu.VMEM
SMEM = pltpu.SMEM


def phase_angle_parts(points):
    index = jnp.arange(points, dtype=jnp.int32)
    windings = index[:, None] * index[None, :] % points
    angles = windings.astype(F32) * (2.0 * math.pi / points)
    return (jnp.cos(angles), jnp.sin(angles))


def row_table_of(points):
    cosine, sine_part = phase_angle_parts(points)
    upper_rows = jnp.concatenate([cosine, -sine_part], 1)
    lower_rows = jnp.concatenate([sine_part, cosine], 1)
    return jnp.concatenate([upper_rows, lower_rows], 0).astype(BF16)


def pack_kernel(pairs_ref, half_ref, vir_ref, occ_ref, out_ref, spread):
    nv = vir_ref.shape[0]
    rows = out_ref.shape[1]
    spread[...] = jnp.zeros_like(spread)

    def put(block, row_of):
        turned = block.astype(F32).T
        for o in range(4):
            lanes = [turned[32 * t : 32 * t + 32, 32 * o : 32 * o + 32] for t in range(4)]
            spread[pl.ds(row_of(o), 32, stride=rows), :] = jnp.concatenate(lanes, 1)

    for g in range(nv // 4):
        put(vir_ref[4 * g : 4 * g + 4].reshape(128, 128), lambda o: 4 * g + o)
    put(occ_ref[...].reshape(128, 128), lambda o: nv + 4 * half_ref[0] + o)
    for c in range(2):
        spread[pl.ds(nv + 8 + c, 32, stride=rows), :] = jnp.full((32, 128), pairs_ref[0, c], jnp.int32).astype(F32)
    out_ref[...] = spread[...].reshape(out_ref.shape).astype(BF16)


def pack(virtual, occupied, pairs, half):
    nv = virtual.shape[0]
    rows = nv + 16
    return pl.pallas_call(
        pack_kernel,
        out_shape=jax.ShapeDtypeStruct((32, rows, 128), BF16),
        in_specs=[pl.BlockSpec(memory_space=SMEM)] * 2 + [pl.BlockSpec(memory_space=VMEM)] * 2,
        out_specs=pl.BlockSpec(memory_space=VMEM),
        scratch_shapes=[pltpu.VMEM((32 * rows, 128), F32)],
        name="pack",
    )(pairs, half, virtual, occupied)


def select_kernel(table_ref, got_ref, out_ref):
    nq = table_ref.shape[0]
    nv = got_ref.shape[1] - 16
    for q in range(nq):
        k1, k2 = table_ref[q, 0], table_ref[q, 1]
        first, second = got_ref[2 * k2, :nv], got_ref[2 * k2 + 1, :nv]
        occ = got_ref[2 * k1, nv:].astype(F32) + got_ref[2 * k1 + 1, nv:].astype(F32)
        occ = occ.astype(BF16)
        for g in range(2):
            out_ref[2 * q + g, :nv] = first
            out_ref[2 * q + g, nv : 2 * nv] = second
            out_ref[2 * q + g, 2 * nv :] = occ


def select(table, got):
    pieces, rows, lanes = got.shape
    nv = rows - 16
    return pl.pallas_call(
        select_kernel,
        out_shape=jax.ShapeDtypeStruct((pieces, 2 * nv + 16, lanes), BF16),
        in_specs=[pl.BlockSpec(memory_space=SMEM), pl.BlockSpec(memory_space=VMEM)],
        out_specs=pl.BlockSpec(memory_space=VMEM),
        name="select",
    )(table, got)


def weight_kernel(turn_ref, column_ref, occ_ref, spread_ref, cos_ref, sin_ref, out_ref):
    def step(yp, carry):
        occ = jnp.concatenate([occ_ref[turn_ref[m], yp].astype(F32) for m in range(4)], 0).astype(BF16)
        wide = lax.dot_general(occ, spread_ref[...], (((0,), (0,)), ((), ())), preferred_element_type=F32)
        for g in range(2):
            for u in range(2):
                c, s = column_ref[0, 32 * u + yp], column_ref[1, 32 * u + yp]
                ac, as_ = cos_ref[g], sin_ref[g]
                tr = ac * c - as_ * s
                ti = as_ * c + ac * s
                real = wide[32 * u : 32 * u + 32, 128 * g : 128 * g + 128]
                imag = wide[64 + 32 * u : 96 + 32 * u, 128 * g : 128 * g + 128]
                wr = (real * tr + imag * ti).astype(BF16)
                wi = real * ti - imag * tr
                base = 128 * g + 32 * u
                out_ref[yp, base : base + 32, :128] = wr
                out_ref[yp, base : base + 32, 128:] = wi.astype(BF16)
                out_ref[yp, base + 64 : base + 96, :128] = (-wi).astype(BF16)
                out_ref[yp, base + 64 : base + 96, 128:] = wr
        return carry

    lax.fori_loop(0, 32, step, 0, unroll=2)


def weights_of(turn, column, occ, spread, cosine, sine_part):
    return pl.pallas_call(
        weight_kernel,
        out_shape=jax.ShapeDtypeStruct((32, 256, 256), BF16),
        in_specs=[pl.BlockSpec(memory_space=SMEM)] * 2 + [pl.BlockSpec(memory_space=VMEM)] * 4,
        out_specs=pl.BlockSpec(memory_space=VMEM),
        compiler_params=pltpu.CompilerParams(vmem_limit_bytes=24 << 20),
        cost_estimate=pl.CostEstimate(flops=32 * 2 * 128 * 32 * 256, bytes_accessed=6 << 20, transcendentals=0),
        name="weights",
    )(turn, column, occ, spread, cosine, sine_part)


def chunk_kernel(place_ref, *refs):
    *vir_refs, weight_ref, row_ref, scale_ref = refs[:-3]
    _, out_ref, total = refs[-3:]
    na = vir_refs[0].shape[1] // 2
    lane = lax.broadcasted_iota(jnp.int32, (na, 256), 1)
    upper = (lane // 32) % 2 == 0
    done = 0
    for vir_ref in vir_refs:
        def first(step, carry, vir_ref=vir_ref, done=done):
            yp = done + step
            both = jnp.concatenate([vir_ref[step, :na], vir_ref[step, na:]], 1)
            nought = jnp.zeros_like(both)
            split = jnp.concatenate([jnp.where(upper, both, nought), jnp.where(upper, nought, both)], 0)
            sums = jnp.dot(split, weight_ref[yp], preferred_element_type=F32)
            for u in range(2):
                for c in range(2):
                    total[c, pl.ds(32 * u + yp, na, stride=64), :] = sums[na * u : na * u + na, 128 * c : 128 * c + 128]
            return carry

        lax.fori_loop(0, vir_ref.shape[0], first, 0, unroll=4)
        done += vir_ref.shape[0]

    def second(a, carry):
        spot = pl.ds(pl.multiple_of(a * 64, 64), 64)
        left = jnp.concatenate([total[0, spot, :], total[1, spot, :]], 0).astype(BF16)
        result = lax.dot_general(left, row_ref[...], (((0,), (0,)), ((), ())), preferred_element_type=F32)
        result = result.reshape(16, 8, 128) * scale_ref[...][None]
        out_ref[:, a] = result.astype(BF16)
        return carry

    lax.fori_loop(0, na, second, 0, unroll=4)


def chunk(place, virs, weights, row_table, scale, out):
    na = virs[0].shape[1] // 2
    whole = lambda a: pl.BlockSpec(a.shape, lambda g, place: (0,) * a.ndim)
    args = [*virs, weights, row_table, scale]
    return pl.pallas_call(
        chunk_kernel,
        out_shape=jax.ShapeDtypeStruct(out.shape, BF16),
        grid_spec=pltpu.PrefetchScalarGridSpec(
            num_scalar_prefetch=1,
            grid=(1,),
            in_specs=[whole(a) for a in args] + [pl.BlockSpec(memory_space=pl.ANY)],
            out_specs=pl.BlockSpec((16, na, 8, 128), lambda g, place: (0, place[0], 0, 0)),
            scratch_shapes=[pltpu.VMEM((2, na * 64, 128), F32)],
        ),
        input_output_aliases={len(args) + 1: 0},
        compiler_params=pltpu.CompilerParams(vmem_limit_bytes=24 << 20),
        cost_estimate=pl.CostEstimate(
            flops=2 * (32 * 64 * 256 * 256 + na * 128 * 128 * 128), bytes_accessed=6 << 20, transcendentals=0
        ),
        name="chunk",
    )(place, *args, out)


def empty_kernel(out_ref):
    pass


def empty(shape):
    return pl.pallas_call(
        empty_kernel,
        out_shape=jax.ShapeDtypeStruct(shape, BF16),
        out_specs=pl.BlockSpec(memory_space=pl.ANY),
        name="empty",
    )()


def spread_table():
    table = np.zeros((4, 2, 4, 2, 16, 8), np.float32)
    for m in range(4):
        for g in range(2):
            for o in range(4):
                table[m, g, o, g, 4 * m + o, :] = 1.0
    return jnp.asarray(table.reshape(32, 256), BF16)


def on_device(occupied, virtual, coulomb, transfer_pairs, shifts):
    points = 64
    z, half = lax.axis_index("kp"), lax.axis_index("ga")
    packed = pack(virtual[0], occupied[0], transfer_pairs, half.reshape(1))
    got = lax.all_to_all(packed, ("ka", "ga"), 0, 0, tiled=False)
    table = got.reshape(16, 2, -1, 128)[:, 0, 40:42, 0].astype(jnp.int32)
    mine = lax.all_to_all(select(table, got), ("ka", "ga"), 0, 0, tiled=False)
    vir, occ = mine[:, :64], mine[:, 64:72]

    grid = jnp.arange(points, dtype=jnp.int32)
    cosine, sine_part = phase_angle_parts(points)
    planes = 8 * z + jnp.arange(8, dtype=jnp.int32)
    col_cos = jnp.take(cosine, planes, axis=0).astype(BF16).astype(F32).T
    col_sin = jnp.take(sine_part, planes, axis=0).astype(BF16).astype(F32).T
    turn_x = ((shifts[0, 0] * grid) % points).astype(F32) * (2.0 * math.pi / points)
    turn_y = ((shifts[0, 1] * grid) % points).astype(F32) * (2.0 * math.pi / points)
    cx, sx = jnp.cos(turn_x)[:, None], -jnp.sin(turn_x)[:, None]
    tab_cos = jnp.tile(col_cos * cx + col_sin * sx, (1, 16)).reshape(2, 32, 128)
    tab_sin = jnp.tile(col_cos * sx - col_sin * cx, (1, 16)).reshape(2, 32, 128)
    column = jnp.stack([jnp.cos(turn_y), -jnp.sin(turn_y)])
    scale = lax.dynamic_slice_in_dim(coulomb[0], 8 * z, 8, 0)
    scale = jnp.concatenate([scale, scale], 1) * (1.0 / points)
    row_table = row_table_of(points)

    forward = [(i, (i + 1) % 8) for i in range(8)]
    backward = [(i, (i - 1) % 8) for i in range(8)]
    occs = {0: occ}
    for s in range(1, 5):
        occs[s] = lax.ppermute(occs[s - 1], "kp", forward)
        if s < 4:
            occs[-s] = lax.ppermute(occs[-(s - 1)], "kp", backward)
    stacked = jnp.stack([occs[r if r <= 4 else r - 8] for r in range(8)])
    turn = (z - (4 * half + jnp.arange(4, dtype=jnp.int32))) % 8
    weights = weights_of(turn, column, stacked, spread_table(), tab_cos, tab_sin)

    out = empty((16, 256, 8, 128))
    out = chunk((z % 8).reshape(1), [vir], weights, row_table, scale, out)
    ahead = behind = vir
    for s in range(1, 4):
        ahead = lax.ppermute(ahead, "kp", forward)
        behind = lax.ppermute(behind, "kp", backward)
        out = chunk(((z - s) % 8).reshape(1), [ahead], weights, row_table, scale, out)
        out = chunk(((z + s) % 8).reshape(1), [behind], weights, row_table, scale, out)
    lower = lax.ppermute(ahead[:16], "kp", forward)
    higher = lax.ppermute(behind[16:], "kp", backward)
    out = chunk(((z + 4) % 8).reshape(1), [lower, higher], weights, row_table, scale, out)
    return out[None]


def solution(mesh):
    in_specs = (
        P("ka", "kp", "ga", None),
        P("ka", "kp", "ga", None),
        P("ka", None, None),
        P("ka", None),
        P("ka", None),
    )
    out_specs = P("ka", "ga", None, "kp", None)
    return jax.shard_map(
        on_device, mesh=mesh, in_specs=in_specs, out_specs=out_specs, check_vma=False
    )
```

```python
import math

import jax
import jax.numpy as jnp
import numpy as np
from jax import lax
from jax.experimental import pallas as pl
from jax.experimental.pallas import tpu as pltpu
from jax.sharding import PartitionSpec as P

F32 = jnp.float32
BF16 = jnp.bfloat16
VMEM = pltpu.VMEM
SMEM = pltpu.SMEM


def phase_angle_parts(points):
    index = jnp.arange(points, dtype=jnp.int32)
    windings = index[:, None] * index[None, :] % points
    angles = windings.astype(F32) * (2.0 * math.pi / points)
    return (jnp.cos(angles), jnp.sin(angles))


def row_table_of(points):
    cosine, sine_part = phase_angle_parts(points)
    upper_rows = jnp.concatenate([cosine, -sine_part], 1)
    lower_rows = jnp.concatenate([sine_part, cosine], 1)
    return jnp.concatenate([upper_rows, lower_rows], 0).astype(BF16)


def pack_kernel(*refs):
    pairs_ref, orb_ref, out_ref, spread = refs if len(refs) == 4 else (None, *refs)
    norb = orb_ref.shape[0]

    for g in range(norb // 4):
        turned = orb_ref[4 * g : 4 * g + 4].reshape(128, 128).astype(F32).T
        for o in range(4):
            lanes = [turned[32 * t : 32 * t + 32, 32 * o : 32 * o + 32] for t in range(4)]
            spread[pl.ds(4 * g + o, 32, stride=norb), :] = jnp.concatenate(lanes, 1)
    out_ref[:, : 2 * norb] = spread[...].reshape(16, 2 * norb, 128).astype(BF16)
    if pairs_ref is not None:
        row = lax.broadcasted_iota(jnp.int32, (16, 16, 128), 1)
        told = jnp.where(row == 0, pairs_ref[0, 0], jnp.where(row == 1, pairs_ref[0, 1], 0))
        out_ref[:, 2 * norb :] = told.astype(F32).astype(BF16)


def pack(orbitals, pairs=None):
    norb = orbitals.shape[0]
    told = [] if pairs is None else [pairs]
    return pl.pallas_call(
        pack_kernel,
        out_shape=jax.ShapeDtypeStruct((16, 2 * norb + 16 * len(told), 128), BF16),
        in_specs=[pl.BlockSpec(memory_space=SMEM)] * len(told) + [pl.BlockSpec(memory_space=VMEM)],
        out_specs=pl.BlockSpec(memory_space=VMEM),
        scratch_shapes=[pltpu.VMEM((32 * norb, 128), F32)],
        name="pack",
    )(*told, orbitals)


def pick_virtual_kernel(table_ref, got_ref, out_ref):
    for q in range(16):
        out_ref[q] = got_ref[table_ref[q, 1], :64]


def pick_occupied_kernel(table_ref, got_ref, out_ref):
    for q in range(16):
        for g in range(2):
            for u in range(2):
                start = 32 * u + 16 * g
                out_ref[2 * q + g, 16 * u : 16 * u + 16] = got_ref[table_ref[q, 0], start : start + 16]


def pick(kernel, table, got, shape):
    return pl.pallas_call(
        kernel,
        out_shape=jax.ShapeDtypeStruct(shape, BF16),
        in_specs=[pl.BlockSpec(memory_space=SMEM), pl.BlockSpec(memory_space=VMEM)],
        out_specs=pl.BlockSpec(memory_space=VMEM),
        name="pick",
    )(table, got)


def weight_kernel(half_ref, column_ref, occ_ref, spread_ref, cos_ref, sin_ref, out_ref):
    half = half_ref[0]

    def step(yp, carry):
        piece, odd = yp // 2, yp % 2
        rows = pl.ds(pl.multiple_of(16 * odd, 16), 16)
        occ = jnp.concatenate([occ_ref[2 * piece + half, rows], occ_ref[2 * piece + 1 - half, rows]], 0)
        wide = lax.dot_general(occ, spread_ref[...], (((0,), (0,)), ((), ())), preferred_element_type=F32)
        for g in range(2):
            ac, as_ = cos_ref[g], sin_ref[g]
            for u in range(2):
                c, s = column_ref[0, 32 * u + yp], column_ref[1, 32 * u + yp]
                tr = ac * c - as_ * s
                ti = as_ * c + ac * s
                real = wide[32 * u : 32 * u + 32, 128 * g : 128 * g + 128]
                imag = wide[64 + 32 * u : 96 + 32 * u, 128 * g : 128 * g + 128]
                wr = (real * tr + imag * ti).astype(BF16)
                wi = real * ti - imag * tr
                base = 128 * g + 32 * u
                out_ref[yp, base : base + 32, :128] = wr
                out_ref[yp, base : base + 32, 128:] = wi.astype(BF16)
                out_ref[yp, base + 64 : base + 96, :128] = (-wi).astype(BF16)
                out_ref[yp, base + 64 : base + 96, 128:] = wr
        return carry

    lax.fori_loop(0, 32, step, 0, unroll=8)


def weights_of(half, column, occ, spread, cosine, sine_part):
    return pl.pallas_call(
        weight_kernel,
        out_shape=jax.ShapeDtypeStruct((32, 256, 256), BF16),
        in_specs=[pl.BlockSpec(memory_space=SMEM)] * 2 + [pl.BlockSpec(memory_space=VMEM)] * 4,
        out_specs=pl.BlockSpec(memory_space=VMEM),
        compiler_params=pltpu.CompilerParams(vmem_limit_bytes=24 << 20),
        cost_estimate=pl.CostEstimate(flops=32 * 2 * 128 * 32 * 256, bytes_accessed=6 << 20, transcendentals=0),
        name="weights",
    )(half, column, occ, spread, cosine, sine_part)


def chunk_kernel(place_ref, *refs):
    vir_refs, (weight_ref, row_ref, scale_ref, _, out_ref, total) = refs[:-6], refs[-6:]
    na = vir_refs[0].shape[1]
    lane = lax.broadcasted_iota(jnp.int32, (na, 256), 1)
    upper = (lane // 32) % 2 == 0
    yp = 0
    for own_ref, other_ref in zip(vir_refs[0::2], vir_refs[1::2]):
        for step in range(own_ref.shape[0]):
            both = jnp.concatenate([own_ref[step], other_ref[step]], 1)
            nought = jnp.zeros_like(both)
            split = jnp.concatenate([jnp.where(upper, both, nought), jnp.where(upper, nought, both)], 0)
            sums = jnp.dot(split, weight_ref[yp], preferred_element_type=F32)
            for u in range(2):
                for c in range(2):
                    total[c, pl.ds(32 * u + yp, na, stride=64), :] = sums[na * u : na * u + na, 128 * c : 128 * c + 128]
            yp += 1

    for a in range(na):
        left = jnp.concatenate([total[c, 64 * a : 64 * a + 64, :] for c in range(2)], 0).astype(BF16)
        result = lax.dot_general(left, row_ref[...], (((0,), (0,)), ((), ())), preferred_element_type=F32)
        out_ref[:, a] = (result.reshape(16, 8, 128) * scale_ref[...][None]).astype(BF16)


def chunk(place, virs, weights, row_table, scale, out):
    na = virs[0].shape[1]
    whole = lambda a: pl.BlockSpec(a.shape, lambda g, place: (0,) * a.ndim)
    args = [*virs, weights, row_table, scale]
    return pl.pallas_call(
        chunk_kernel,
        out_shape=jax.ShapeDtypeStruct(out.shape, BF16),
        grid_spec=pltpu.PrefetchScalarGridSpec(
            num_scalar_prefetch=1,
            grid=(1,),
            in_specs=[whole(a) for a in args] + [pl.BlockSpec(memory_space=pl.ANY)],
            out_specs=pl.BlockSpec((16, na, 8, 128), lambda g, place: (0, place[0], 0, 0)),
            scratch_shapes=[pltpu.VMEM((2, na * 64, 128), F32)],
        ),
        input_output_aliases={len(args) + 1: 0},
        compiler_params=pltpu.CompilerParams(vmem_limit_bytes=24 << 20),
        cost_estimate=pl.CostEstimate(
            flops=2 * (32 * 64 * 256 * 256 + na * 128 * 128 * 128), bytes_accessed=6 << 20, transcendentals=0
        ),
        name="chunk",
    )(place, *args, out)


def empty_kernel(out_ref):
    pass


def empty(shape):
    return pl.pallas_call(
        empty_kernel,
        out_shape=jax.ShapeDtypeStruct(shape, BF16),
        out_specs=pl.BlockSpec(memory_space=pl.ANY),
        name="empty",
    )()


def spread_table():
    table = np.zeros((2, 16, 2, 16, 8), np.float32)
    for g in range(2):
        for i in range(16):
            table[g, i, g, i, :] = 1.0
    return jnp.asarray(table.reshape(32, 256), BF16)


def on_device(occupied, virtual, coulomb, transfer_pairs, shifts):
    points = 64
    z, half = lax.axis_index("kp"), lax.axis_index("ga")
    shared = lax.all_to_all(jnp.broadcast_to(occupied, (8, 4, 32, 128)), "kp", 0, 0, tiled=False)
    got = lax.all_to_all(pack(virtual[0], transfer_pairs), "ka", 0, 0, tiled=False)
    got_occ = lax.all_to_all(pack(shared.reshape(32, 32, 128)), "ka", 0, 0, tiled=False)
    table = got[:, 64:66, 0].astype(jnp.int32)
    own = lax.all_to_all(pick(pick_virtual_kernel, table, got, (16, 64, 128)), "ka", 0, 0, tiled=False)
    own = own.reshape(32, 32, 128)
    occ = pick(pick_occupied_kernel, table, got_occ, (32, 32, 128))
    occ = lax.all_to_all(occ, ("ka", "ga"), 0, 0, tiled=False)

    grid = jnp.arange(points, dtype=jnp.int32)
    cosine, sine_part = phase_angle_parts(points)
    planes = 8 * z + jnp.arange(8, dtype=jnp.int32)
    col_cos = jnp.take(cosine, planes, axis=0).astype(BF16).astype(F32).T
    col_sin = jnp.take(sine_part, planes, axis=0).astype(BF16).astype(F32).T
    turn_x = ((shifts[0, 0] * grid) % points).astype(F32) * (2.0 * math.pi / points)
    turn_y = ((shifts[0, 1] * grid) % points).astype(F32) * (2.0 * math.pi / points)
    cx, sx = jnp.cos(turn_x)[:, None], -jnp.sin(turn_x)[:, None]
    tab_cos = jnp.tile(col_cos * cx + col_sin * sx, (1, 16)).reshape(2, 32, 128)
    tab_sin = jnp.tile(col_cos * sx - col_sin * cx, (1, 16)).reshape(2, 32, 128)
    column = jnp.stack([jnp.cos(turn_y), -jnp.sin(turn_y)])
    scale = lax.dynamic_slice_in_dim(coulomb[0], 8 * z, 8, 0)
    scale = jnp.concatenate([scale, scale], 1) * (1.0 / points)
    row_table = row_table_of(points)

    forward = [(i, (i + 1) % 8) for i in range(8)]
    backward = [(i, (i - 1) % 8) for i in range(8)]
    tab_cos = jnp.where(half == 0, tab_cos, tab_cos[::-1])
    tab_sin = jnp.where(half == 0, tab_sin, tab_sin[::-1])
    weights = weights_of(half.reshape(1), column, occ, spread_table(), tab_cos, tab_sin)

    def place(s):
        return ((z - s) % 8).reshape(1)

    other = lax.ppermute(own, "ga", [(0, 1), (1, 0)])
    out = empty((16, 256, 8, 128))
    out = chunk(place(0), [own, other], weights, row_table, scale, out)
    ahead = behind = [own, other]
    for s in range(1, 4):
        ahead = [lax.ppermute(v, "kp", forward) for v in ahead]
        behind = [lax.ppermute(v, "kp", backward) for v in behind]
        out = chunk(place(s), ahead, weights, row_table, scale, out)
        out = chunk(place(-s), behind, weights, row_table, scale, out)
    lower = [lax.ppermute(v[:16], "kp", forward) for v in ahead]
    higher = [lax.ppermute(v[16:], "kp", backward) for v in behind]
    out = chunk(place(4), lower + higher, weights, row_table, scale, out)
    return out[None]


def solution(mesh):
    in_specs = (
        P("ka", "kp", "ga", None),
        P("ka", "kp", "ga", None),
        P("ka", None, None),
        P("ka", None),
        P("ka", None),
    )
    out_specs = P("ka", "ga", None, "kp", None)
    return jax.shard_map(
        on_device, mesh=mesh, in_specs=in_specs, out_specs=out_specs, check_vma=False
    )
```

```python
import functools
import math

import jax
import jax.numpy as jnp
import numpy as np
from jax import lax
from jax.experimental import pallas as pl
from jax.experimental.pallas import tpu as pltpu
from jax.sharding import PartitionSpec as P

F32 = jnp.float32
BF16 = jnp.bfloat16
VMEM = pltpu.VMEM
SMEM = pltpu.SMEM


def phase_angle_parts(points):
    index = jnp.arange(points, dtype=jnp.int32)
    windings = index[:, None] * index[None, :] % points
    angles = windings.astype(F32) * (2.0 * math.pi / points)
    return (jnp.cos(angles), jnp.sin(angles))


def row_table_of(points):
    cosine, sine_part = phase_angle_parts(points)
    upper_rows = jnp.concatenate([cosine, -sine_part], 1)
    lower_rows = jnp.concatenate([sine_part, cosine], 1)
    return jnp.concatenate([upper_rows, lower_rows], 0).astype(BF16)


def turn_orbitals(orb_ref, spread):
    norb = orb_ref.shape[0]
    for g in range(norb // 4):
        turned = orb_ref[4 * g : 4 * g + 4].reshape(128, 128).astype(F32).T
        for o in range(4):
            lanes = [turned[32 * t : 32 * t + 32, 32 * o : 32 * o + 32] for t in range(4)]
            spread[pl.ds(4 * g + o, 32, stride=norb), :] = jnp.concatenate(lanes, 1)
    return spread[...].reshape(16, 2 * norb, 128).astype(BF16)


def open_kernel(pairs_ref, vir_ref, occ_ref, out_ref, copies_ref, spread):
    for z in range(8):
        copies_ref[z] = occ_ref[...]
    out_ref[:, :64] = turn_orbitals(vir_ref, spread)
    row = lax.broadcasted_iota(jnp.int32, (16, 16, 128), 1)
    told = jnp.where(row == 0, pairs_ref[0, 0], jnp.where(row == 1, pairs_ref[0, 1], 0))
    out_ref[:, 64:] = told.astype(F32).astype(BF16)


def open_up(pairs, virtual, occupied):
    return pl.pallas_call(
        open_kernel,
        out_shape=[jax.ShapeDtypeStruct((16, 80, 128), BF16), jax.ShapeDtypeStruct((8, *occupied.shape), BF16)],
        in_specs=[pl.BlockSpec(memory_space=SMEM)] + [pl.BlockSpec(memory_space=VMEM)] * 2,
        out_specs=[pl.BlockSpec(memory_space=VMEM)] * 2,
        scratch_shapes=[pltpu.VMEM((1024, 128), F32)],
        name="open_up",
    )(pairs, virtual, occupied)


def middle_kernel(second_ref, got_ref, shared_ref, out_ref, spread):
    out_ref[:, 64:] = turn_orbitals(shared_ref, spread)
    for q in range(16):
        out_ref[q, :64] = got_ref[second_ref[q], :64]


def middle(second, got, shared):
    return pl.pallas_call(
        middle_kernel,
        out_shape=jax.ShapeDtypeStruct((16, 128, 128), BF16),
        in_specs=[pl.BlockSpec(memory_space=SMEM)] + [pl.BlockSpec(memory_space=VMEM)] * 2,
        out_specs=pl.BlockSpec(memory_space=VMEM),
        scratch_shapes=[pltpu.VMEM((1024, 128), F32)],
        name="middle",
    )(second, got, shared)


def pick_kernel(first_ref, got_ref, out_ref):
    for q in range(16):
        for g in range(2):
            for u in range(2):
                start = 64 + 32 * u + 16 * g
                out_ref[2 * q + g, 16 * u : 16 * u + 16] = got_ref[first_ref[q], start : start + 16]


def pick_occupied(first, got):
    return pl.pallas_call(
        pick_kernel,
        out_shape=jax.ShapeDtypeStruct((32, 32, 128), BF16),
        in_specs=[pl.BlockSpec(memory_space=SMEM), pl.BlockSpec(memory_space=VMEM)],
        out_specs=pl.BlockSpec(memory_space=VMEM),
        name="pick_occupied",
    )(first, got)


def weight_kernel(half_ref, column_ref, occ_ref, spread_ref, cos_ref, sin_ref, out_ref):
    half = half_ref[0]

    def step(yp, carry):
        piece, odd = yp // 2, yp % 2
        rows = pl.ds(pl.multiple_of(16 * odd, 16), 16)
        occ = jnp.concatenate([occ_ref[2 * piece + half, rows], occ_ref[2 * piece + 1 - half, rows]], 0)
        wide = lax.dot_general(occ, spread_ref[...], (((0,), (0,)), ((), ())), preferred_element_type=F32)
        for g in range(2):
            ac, as_ = cos_ref[g], sin_ref[g]
            for u in range(2):
                c, s = column_ref[0, 32 * u + yp], column_ref[1, 32 * u + yp]
                tr = ac * c - as_ * s
                ti = as_ * c + ac * s
                real = wide[32 * u : 32 * u + 32, 128 * g : 128 * g + 128]
                imag = wide[64 + 32 * u : 96 + 32 * u, 128 * g : 128 * g + 128]
                wr = (real * tr + imag * ti).astype(BF16)
                wi = real * ti - imag * tr
                base = 128 * g + 32 * u
                out_ref[yp, base : base + 32, :128] = wr
                out_ref[yp, base : base + 32, 128:] = wi.astype(BF16)
                out_ref[yp, base + 64 : base + 96, :128] = (-wi).astype(BF16)
                out_ref[yp, base + 64 : base + 96, 128:] = wr
        return carry

    lax.fori_loop(0, 32, step, 0, unroll=8)


def weights_of(half, column, occ, spread, cosine, sine_part):
    return pl.pallas_call(
        weight_kernel,
        out_shape=jax.ShapeDtypeStruct((32, 256, 256), BF16),
        in_specs=[pl.BlockSpec(memory_space=SMEM)] * 2 + [pl.BlockSpec(memory_space=VMEM)] * 4,
        out_specs=pl.BlockSpec(memory_space=VMEM),
        compiler_params=pltpu.CompilerParams(vmem_limit_bytes=24 << 20),
        cost_estimate=pl.CostEstimate(flops=32 * 2 * 128 * 32 * 256, bytes_accessed=6 << 20, transcendentals=0),
        name="weights",
    )(half, column, occ, spread, cosine, sine_part)


def chunk_kernel(parts, place_ref, *refs):
    vir_refs, (weight_ref, row_ref, scale_ref, _, out_ref, total, ready, sems) = refs[:-8], refs[-8:]
    lane = lax.broadcasted_iota(jnp.int32, (32, 256), 1)
    upper = (lane // 32) % 2 == 0
    copies = []
    for n, part in enumerate(parts):
        here = vir_refs[: 2 * part]
        vir_refs = vir_refs[2 * part :]
        yp = 0
        for own_ref, other_ref in zip(here[0::2], here[1::2]):
            for step in range(own_ref.shape[0]):
                both = jnp.concatenate([own_ref[step], other_ref[step]], 1)
                nought = jnp.zeros_like(both)
                split = jnp.concatenate([jnp.where(upper, both, nought), jnp.where(upper, nought, both)], 0)
                sums = jnp.dot(split, weight_ref[yp], preferred_element_type=F32)
                for u in range(2):
                    for c in range(2):
                        block = sums[32 * u : 32 * u + 32, 128 * c : 128 * c + 128]
                        total[n, c, pl.ds(32 * u + yp, 32, stride=64), :] = block
                yp += 1

        for a in range(32):
            left = jnp.concatenate([total[n, c, 64 * a : 64 * a + 64, :] for c in range(2)], 0).astype(BF16)
            result = lax.dot_general(left, row_ref[...], (((0,), (0,)), ((), ())), preferred_element_type=F32)
            ready[n, :, a] = (result.reshape(16, 8, 128) * scale_ref[...][None]).astype(BF16)
            if a % 8 == 7:
                copy = pltpu.make_async_copy(
                    ready.at[n, :, pl.ds(a - 7, 8)],
                    out_ref.at[:, pl.ds(32 * place_ref[n] + (a - 7), 8)],
                    sems.at[n, a // 8],
                )
                copy.start()
                copies.append(copy)
    for copy in copies:
        copy.wait()


def chunk(places, virs, weights, row_table, scale, out):
    n = len(virs)
    args = [v for vir in virs for v in vir] + [weights, row_table, scale]
    return pl.pallas_call(
        functools.partial(chunk_kernel, [len(vir) // 2 for vir in virs]),
        out_shape=jax.ShapeDtypeStruct(out.shape, BF16),
        in_specs=[pl.BlockSpec(memory_space=SMEM)]
        + [pl.BlockSpec(memory_space=VMEM)] * len(args)
        + [pl.BlockSpec(memory_space=pl.ANY)],
        out_specs=pl.BlockSpec(memory_space=pl.ANY),
        scratch_shapes=[
            pltpu.VMEM((n, 2, 32 * 64, 128), F32),
            pltpu.VMEM((n, 16, 32, 8, 128), BF16),
            pltpu.SemaphoreType.DMA((n, 4)),
        ],
        input_output_aliases={len(args) + 1: 0},
        compiler_params=pltpu.CompilerParams(vmem_limit_bytes=24 << 20),
        cost_estimate=pl.CostEstimate(flops=n << 31, bytes_accessed=n << 20, transcendentals=0),
        name="chunk",
    )(jnp.stack(places), *args, out)


def empty_kernel(out_ref):
    pass


def empty(shape):
    return pl.pallas_call(
        empty_kernel,
        out_shape=jax.ShapeDtypeStruct(shape, BF16),
        out_specs=pl.BlockSpec(memory_space=pl.ANY),
        name="empty",
    )()


def spread_table():
    table = np.zeros((2, 16, 2, 16, 8), np.float32)
    for g in range(2):
        for i in range(16):
            table[g, i, g, i, :] = 1.0
    return jnp.asarray(table.reshape(32, 256), BF16)


def on_device(occupied, virtual, coulomb, transfer_pairs, shifts):
    points = 64
    z, half = lax.axis_index("kp"), lax.axis_index("ga")
    packed, copies = open_up(transfer_pairs, virtual[0], occupied[0])
    got = lax.all_to_all(packed, "ka", 0, 0, tiled=False)
    shared = lax.all_to_all(copies, "kp", 0, 0, tiled=False).reshape(32, 32, 128)
    first, second = got[:, 64, 0].astype(jnp.int32), got[:, 65, 0].astype(jnp.int32)
    mine = lax.all_to_all(middle(second, got, shared), "ka", 0, 0, tiled=False)
    own = mine[:, :64].reshape(32, 32, 128)
    occ = lax.all_to_all(pick_occupied(first, mine), ("ka", "ga"), 0, 0, tiled=False)

    grid = jnp.arange(points, dtype=jnp.int32)
    cosine, sine_part = phase_angle_parts(points)
    planes = 8 * z + jnp.arange(8, dtype=jnp.int32)
    col_cos = jnp.take(cosine, planes, axis=0).astype(BF16).astype(F32).T
    col_sin = jnp.take(sine_part, planes, axis=0).astype(BF16).astype(F32).T
    turn_x = ((shifts[0, 0] * grid) % points).astype(F32) * (2.0 * math.pi / points)
    turn_y = ((shifts[0, 1] * grid) % points).astype(F32) * (2.0 * math.pi / points)
    cx, sx = jnp.cos(turn_x)[:, None], -jnp.sin(turn_x)[:, None]
    tab_cos = jnp.tile(col_cos * cx + col_sin * sx, (1, 16)).reshape(2, 32, 128)
    tab_sin = jnp.tile(col_cos * sx - col_sin * cx, (1, 16)).reshape(2, 32, 128)
    column = jnp.stack([jnp.cos(turn_y), -jnp.sin(turn_y)])
    scale = lax.dynamic_slice_in_dim(coulomb[0], 8 * z, 8, 0)
    scale = jnp.concatenate([scale, scale], 1) * (1.0 / points)
    row_table = row_table_of(points)

    forward = [(i, (i + 1) % 8) for i in range(8)]
    backward = [(i, (i - 1) % 8) for i in range(8)]
    tab_cos = jnp.where(half == 0, tab_cos, tab_cos[::-1])
    tab_sin = jnp.where(half == 0, tab_sin, tab_sin[::-1])
    weights = weights_of(half.reshape(1), column, occ, spread_table(), tab_cos, tab_sin)

    def add(shifted, virs, out):
        return chunk([(z - s) % 8 for s in shifted], virs, weights, row_table, scale, out)

    other = lax.ppermute(own, "ga", [(0, 1), (1, 0)])
    out = add([0], [[own, other]], empty((16, 256, 8, 128)))
    ahead = behind = [own, other]
    for s in range(1, 4):
        ahead = [lax.ppermute(v, "kp", forward) for v in ahead]
        behind = [lax.ppermute(v, "kp", backward) for v in behind]
        out = add([s, -s], [ahead, behind], out)
    lower = [lax.ppermute(v[:16], "kp", forward) for v in ahead]
    higher = [lax.ppermute(v[16:], "kp", backward) for v in behind]
    out = add([4], [lower + higher], out)
    return out[None]


def solution(mesh):
    in_specs = (
        P("ka", "kp", "ga", None),
        P("ka", "kp", "ga", None),
        P("ka", None, None),
        P("ka", None),
        P("ka", None),
    )
    out_specs = P("ka", "ga", None, "kp", None)
    return jax.shard_map(
        on_device, mesh=mesh, in_specs=in_specs, out_specs=out_specs, check_vma=False
    )
```

```python
import functools
import math

import jax
import jax.numpy as jnp
import numpy as np
from jax import lax
from jax.experimental import pallas as pl
from jax.experimental.pallas import tpu as pltpu
from jax.sharding import PartitionSpec as P

F32 = jnp.float32
BF16 = jnp.bfloat16
VMEM = pltpu.VMEM
SMEM = pltpu.SMEM


def phase_angle_parts(points):
    index = jnp.arange(points, dtype=jnp.int32)
    windings = index[:, None] * index[None, :] % points
    angles = windings.astype(F32) * (2.0 * math.pi / points)
    return (jnp.cos(angles), jnp.sin(angles))


def row_table_of(points):
    cosine, sine_part = phase_angle_parts(points)
    upper_rows = jnp.concatenate([cosine, -sine_part], 1)
    lower_rows = jnp.concatenate([sine_part, cosine], 1)
    return jnp.concatenate([upper_rows, lower_rows], 0).astype(BF16)


def turn_orbitals(orb_ref, spread):
    norb = orb_ref.shape[0]
    for g in range(norb // 4):
        turned = orb_ref[4 * g : 4 * g + 4].reshape(128, 128).astype(F32).T
        for o in range(4):
            lanes = [turned[32 * t : 32 * t + 32, 32 * o : 32 * o + 32] for t in range(4)]
            spread[pl.ds(4 * g + o, 32, stride=norb), :] = jnp.concatenate(lanes, 1)
    return spread[...].reshape(16, 2 * norb, 128)


def open_kernel(pairs_ref, vir_ref, occ_ref, out_ref, spread, spread_occ):
    out_ref[:, :64] = turn_orbitals(vir_ref, spread).astype(BF16)
    row = lax.broadcasted_iota(jnp.int32, (16, 8, 128), 1)
    told = jnp.where(row == 0, pairs_ref[0, 0], jnp.where(row == 1, pairs_ref[0, 1], 0))
    rest = [turn_orbitals(occ_ref, spread_occ), told.astype(F32)]
    out_ref[:, 64:] = jnp.concatenate(rest, 1).astype(BF16)


def open_up(pairs, virtual, occupied):
    return pl.pallas_call(
        open_kernel,
        out_shape=jax.ShapeDtypeStruct((16, 80, 128), BF16),
        in_specs=[pl.BlockSpec(memory_space=SMEM)] + [pl.BlockSpec(memory_space=VMEM)] * 2,
        out_specs=pl.BlockSpec(memory_space=VMEM),
        scratch_shapes=[pltpu.VMEM((1024, 128), F32), pltpu.VMEM((128, 128), F32)],
        name="open_up",
    )(pairs, virtual, occupied)


def pick_kernel(first_ref, second_ref, got_ref, vir_ref, occ_ref):
    for q in range(16):
        vir_ref[q] = got_ref[second_ref[q], :64]
    for q in range(0, 16, 2):
        two = [got_ref[first_ref[q + n], 64:].astype(F32)[:8] for n in range(2)]
        occ_ref[q // 2] = jnp.concatenate(two, 0).astype(BF16)


def pick(first, second, got):
    return pl.pallas_call(
        pick_kernel,
        out_shape=[jax.ShapeDtypeStruct((16, 64, 128), BF16), jax.ShapeDtypeStruct((8, 16, 128), BF16)],
        in_specs=[pl.BlockSpec(memory_space=SMEM)] * 2 + [pl.BlockSpec(memory_space=VMEM)],
        out_specs=[pl.BlockSpec(memory_space=VMEM)] * 2,
        name="pick",
    )(first, second, got)


CAME_BY = ((0, 4), (7, 3), (1, 5), (6, 2))


def deal_kernel(z_ref, *refs):
    got_refs, (out_ref, held) = refs[:4], refs[4:]
    for got_ref, steps in zip(got_refs, CAME_BY):
        for n in range(2):
            held[steps[n]] = got_ref[n].astype(F32)
    for g in range(2):
        for m in range(0, 4, 2):
            sources = [(4 * g + m + n - z_ref[0] + 8) % 8 for n in range(2)]
            for q in range(16):
                spot = 8 * (q % 2)
                rows = jnp.concatenate([held[s, q // 2, spot : spot + 8] for s in sources], 0)
                out_ref[2 * q + g, 8 * m : 8 * m + 16] = rows.astype(BF16)


def deal(z, got):
    return pl.pallas_call(
        deal_kernel,
        out_shape=jax.ShapeDtypeStruct((32, 32, 128), BF16),
        in_specs=[pl.BlockSpec(memory_space=SMEM)] + [pl.BlockSpec(memory_space=VMEM)] * 4,
        out_specs=pl.BlockSpec(memory_space=VMEM),
        scratch_shapes=[pltpu.VMEM((8, 8, 16, 128), F32)],
        name="deal",
    )(z, *got)


def weight_kernel(half_ref, column_ref, occ_ref, spread_ref, cos_ref, sin_ref, out_ref):
    half = half_ref[0]

    def step(yp, carry):
        piece, odd = yp // 2, yp % 2
        occ = jnp.concatenate([occ_ref[2 * piece + half], occ_ref[2 * piece + 1 - half]], 0)
        wide = lax.dot_general(occ, spread_ref[odd], (((0,), (0,)), ((), ())), preferred_element_type=F32)
        for g in range(2):
            ac, as_ = cos_ref[g], sin_ref[g]
            for u in range(2):
                c, s = column_ref[0, 32 * u + yp], column_ref[1, 32 * u + yp]
                tr = ac * c - as_ * s
                ti = as_ * c + ac * s
                real = wide[32 * u : 32 * u + 32, 128 * g : 128 * g + 128]
                imag = wide[64 + 32 * u : 96 + 32 * u, 128 * g : 128 * g + 128]
                wr = (real * tr + imag * ti).astype(BF16)
                wi = real * ti - imag * tr
                base = 128 * g + 32 * u
                out_ref[yp, base : base + 32, :128] = wr
                out_ref[yp, base : base + 32, 128:] = wi.astype(BF16)
                out_ref[yp, base + 64 : base + 96, :128] = (-wi).astype(BF16)
                out_ref[yp, base + 64 : base + 96, 128:] = wr
        return carry

    lax.fori_loop(0, 32, step, 0, unroll=8)


def weights_of(half, column, occ, spread, cosine, sine_part):
    return pl.pallas_call(
        weight_kernel,
        out_shape=jax.ShapeDtypeStruct((32, 256, 256), BF16),
        in_specs=[pl.BlockSpec(memory_space=SMEM)] * 2 + [pl.BlockSpec(memory_space=VMEM)] * 4,
        out_specs=pl.BlockSpec(memory_space=VMEM),
        compiler_params=pltpu.CompilerParams(vmem_limit_bytes=24 << 20),
        cost_estimate=pl.CostEstimate(flops=32 * 2 * 128 * 32 * 256, bytes_accessed=6 << 20, transcendentals=0),
        name="weights",
    )(half, column, occ, spread, cosine, sine_part)


def chunk_kernel(parts, place_ref, *refs):
    vir_refs, (weight_ref, row_ref, scale_ref, _, out_ref, total, ready, sems) = refs[:-8], refs[-8:]
    lane = lax.broadcasted_iota(jnp.int32, (32, 256), 1)
    upper = (lane // 32) % 2 == 0
    copies = []
    for n, part in enumerate(parts):
        here = vir_refs[: 2 * part]
        vir_refs = vir_refs[2 * part :]
        yp = 0
        for own_ref, other_ref in zip(here[0::2], here[1::2]):
            for step in range(own_ref.shape[0]):
                both = jnp.concatenate([own_ref[step], other_ref[step]], 1)
                nought = jnp.zeros_like(both)
                split = jnp.concatenate([jnp.where(upper, both, nought), jnp.where(upper, nought, both)], 0)
                sums = jnp.dot(split, weight_ref[yp], preferred_element_type=F32)
                for u in range(2):
                    for c in range(2):
                        block = sums[32 * u : 32 * u + 32, 128 * c : 128 * c + 128]
                        total[n, c, pl.ds(32 * u + yp, 32, stride=64), :] = block
                yp += 1

        for a in range(32):
            left = jnp.concatenate([total[n, c, 64 * a : 64 * a + 64, :] for c in range(2)], 0).astype(BF16)
            result = lax.dot_general(left, row_ref[...], (((0,), (0,)), ((), ())), preferred_element_type=F32)
            ready[n, :, a] = (result.reshape(16, 8, 128) * scale_ref[...][None]).astype(BF16)
            if a % 8 == 7:
                copy = pltpu.make_async_copy(
                    ready.at[n, :, pl.ds(a - 7, 8)],
                    out_ref.at[:, pl.ds(32 * place_ref[n] + (a - 7), 8)],
                    sems.at[n, a // 8],
                )
                copy.start()
                copies.append(copy)
    for copy in copies:
        copy.wait()


def chunk(places, virs, weights, row_table, scale, out):
    n = len(virs)
    args = [v for vir in virs for v in vir] + [weights, row_table, scale]
    return pl.pallas_call(
        functools.partial(chunk_kernel, [len(vir) // 2 for vir in virs]),
        out_shape=jax.ShapeDtypeStruct(out.shape, BF16),
        in_specs=[pl.BlockSpec(memory_space=SMEM)]
        + [pl.BlockSpec(memory_space=VMEM)] * len(args)
        + [pl.BlockSpec(memory_space=pl.ANY)],
        out_specs=pl.BlockSpec(memory_space=pl.ANY),
        scratch_shapes=[
            pltpu.VMEM((n, 2, 32 * 64, 128), F32),
            pltpu.VMEM((n, 16, 32, 8, 128), BF16),
            pltpu.SemaphoreType.DMA((n, 4)),
        ],
        input_output_aliases={len(args) + 1: 0},
        compiler_params=pltpu.CompilerParams(vmem_limit_bytes=24 << 20),
        cost_estimate=pl.CostEstimate(flops=n << 31, bytes_accessed=n << 20, transcendentals=0),
        name="chunk",
    )(jnp.stack(places), *args, out)


def empty_kernel(out_ref):
    pass


def empty(shape):
    return pl.pallas_call(
        empty_kernel,
        out_shape=jax.ShapeDtypeStruct(shape, BF16),
        out_specs=pl.BlockSpec(memory_space=pl.ANY),
        name="empty",
    )()


def spread_table():
    table = np.zeros((2, 2, 4, 2, 4, 2, 16, 8), np.float32)
    for u in range(2):
        for g in range(2):
            for m in range(4):
                for o in range(4):
                    table[u, g, m, u, o, g, 4 * m + o, :] = 1.0
    return jnp.asarray(table.reshape(2, 64, 256), BF16)


def on_device(occupied, virtual, coulomb, transfer_pairs, shifts):
    points = 64
    z, half = lax.axis_index("kp"), lax.axis_index("ga")
    got = lax.all_to_all(open_up(transfer_pairs, virtual[0], occupied[0]), "ka", 0, 0, tiled=False)
    first, second = got[:, 72, 0].astype(jnp.int32), got[:, 73, 0].astype(jnp.int32)
    picked, occ = pick(first, second, got)
    own = lax.all_to_all(picked, "ka", 0, 0, tiled=False).reshape(32, 32, 128)
    two = jnp.stack([occ, lax.ppermute(occ, "kp", [(i, (i + 4) % 8) for i in range(8)])])
    occ = [two] + [lax.ppermute(two, "kp", [(i, (i + s) % 8) for i in range(8)]) for s in (1, -1, 2)]
    occ = lax.all_to_all(deal(z.reshape(1), occ), ("ka", "ga"), 0, 0, tiled=False)

    grid = jnp.arange(points, dtype=jnp.int32)
    cosine, sine_part = phase_angle_parts(points)
    planes = 8 * z + jnp.arange(8, dtype=jnp.int32)
    col_cos = jnp.take(cosine, planes, axis=0).astype(BF16).astype(F32).T
    col_sin = jnp.take(sine_part, planes, axis=0).astype(BF16).astype(F32).T
    turn_x = ((shifts[0, 0] * grid) % points).astype(F32) * (2.0 * math.pi / points)
    turn_y = ((shifts[0, 1] * grid) % points).astype(F32) * (2.0 * math.pi / points)
    cx, sx = jnp.cos(turn_x)[:, None], -jnp.sin(turn_x)[:, None]
    tab_cos = jnp.tile(col_cos * cx + col_sin * sx, (1, 16)).reshape(2, 32, 128)
    tab_sin = jnp.tile(col_cos * sx - col_sin * cx, (1, 16)).reshape(2, 32, 128)
    column = jnp.stack([jnp.cos(turn_y), -jnp.sin(turn_y)])
    scale = lax.dynamic_slice_in_dim(coulomb[0], 8 * z, 8, 0)
    scale = jnp.concatenate([scale, scale], 1) * (1.0 / points)
    row_table = row_table_of(points)

    forward = [(i, (i + 1) % 8) for i in range(8)]
    backward = [(i, (i - 1) % 8) for i in range(8)]
    tab_cos = jnp.where(half == 0, tab_cos, tab_cos[::-1])
    tab_sin = jnp.where(half == 0, tab_sin, tab_sin[::-1])
    weights = weights_of(half.reshape(1), column, occ, spread_table(), tab_cos, tab_sin)

    def add(shifted, virs, out):
        return chunk([(z - s) % 8 for s in shifted], virs, weights, row_table, scale, out)

    other = lax.ppermute(own, "ga", [(0, 1), (1, 0)])
    out = add([0], [[own, other]], empty((16, 256, 8, 128)))
    ahead = behind = [own, other]
    for s in range(1, 4):
        ahead = [lax.ppermute(v, "kp", forward) for v in ahead]
        behind = [lax.ppermute(v, "kp", backward) for v in behind]
        out = add([s, -s], [ahead, behind], out)
    lower = [lax.ppermute(v[:16], "kp", forward) for v in ahead]
    higher = [lax.ppermute(v[16:], "kp", backward) for v in behind]
    out = add([4], [lower + higher], out)
    return out[None]


def solution(mesh):
    in_specs = (
        P("ka", "kp", "ga", None),
        P("ka", "kp", "ga", None),
        P("ka", None, None),
        P("ka", None),
        P("ka", None),
    )
    out_specs = P("ka", "ga", None, "kp", None)
    return jax.shard_map(
        on_device, mesh=mesh, in_specs=in_specs, out_specs=out_specs, check_vma=False
    )
```

```python
import functools
import math

import jax
import jax.numpy as jnp
import numpy as np
from jax import lax
from jax.experimental import pallas as pl
from jax.experimental.pallas import tpu as pltpu
from jax.sharding import PartitionSpec as P

F32 = jnp.float32
PITCH = 72
BF16 = jnp.bfloat16
VMEM = pltpu.VMEM
SMEM = pltpu.SMEM


def phase_angle_parts(points):
    index = jnp.arange(points, dtype=jnp.int32)
    windings = index[:, None] * index[None, :] % points
    angles = windings.astype(F32) * (2.0 * math.pi / points)
    return (jnp.cos(angles), jnp.sin(angles))


def row_table_of(points):
    cosine, sine_part = phase_angle_parts(points)
    upper_rows = jnp.concatenate([cosine, -sine_part], 1)
    lower_rows = jnp.concatenate([sine_part, cosine], 1)
    return jnp.concatenate([upper_rows, lower_rows], 0).astype(BF16)


def turn_orbitals(orb_ref, spread):
    norb = orb_ref.shape[0]
    pitch = spread.shape[0] // 32
    for g in range(norb // 4):
        turned = orb_ref[4 * g : 4 * g + 4].reshape(128, 128).astype(F32).T
        for o in range(4):
            lanes = [turned[32 * t : 32 * t + 32, 32 * o : 32 * o + 32] for t in range(4)]
            spread[pl.ds(4 * g + o, 32, stride=pitch), :] = jnp.concatenate(lanes, 1)
    rows = [spread[pitch * yp : pitch * yp + norb] for yp in range(32)]
    return jnp.concatenate(rows, 0).reshape(16, 2 * norb, 128)


def open_kernel(pairs_ref, vir_ref, occ_ref, out_ref, spread, spread_occ):
    out_ref[:, :64] = turn_orbitals(vir_ref, spread).astype(BF16)
    row = lax.broadcasted_iota(jnp.int32, (16, 8, 128), 1)
    told = jnp.where(row == 0, pairs_ref[0, 0], jnp.where(row == 1, pairs_ref[0, 1], 0))
    rest = [turn_orbitals(occ_ref, spread_occ), told.astype(F32)]
    out_ref[:, 64:] = jnp.concatenate(rest, 1).astype(BF16)


def open_up(pairs, virtual, occupied):
    return pl.pallas_call(
        open_kernel,
        out_shape=jax.ShapeDtypeStruct((16, 80, 128), BF16),
        in_specs=[pl.BlockSpec(memory_space=SMEM)] + [pl.BlockSpec(memory_space=VMEM)] * 2,
        out_specs=pl.BlockSpec(memory_space=VMEM),
        scratch_shapes=[pltpu.VMEM((32 * 40, 128), F32), pltpu.VMEM((32 * 8, 128), F32)],
        name="open_up",
    )(pairs, virtual, occupied)


def pick_virtual_kernel(second_ref, got_ref, vir_ref):
    for q in range(16):
        vir_ref[q] = got_ref[second_ref[q], :64]


def pick_virtual(second, got):
    return pl.pallas_call(
        pick_virtual_kernel,
        out_shape=jax.ShapeDtypeStruct((16, 64, 128), BF16),
        in_specs=[pl.BlockSpec(memory_space=SMEM), pl.BlockSpec(memory_space=VMEM)],
        out_specs=pl.BlockSpec(memory_space=VMEM),
        name="pick_virtual",
    )(second, got)


def pick_occupied_kernel(first_ref, got_ref, _, occ_ref):
    for q in range(0, 16, 2):
        two = [got_ref[first_ref[q + n], 64:].astype(F32)[:8] for n in range(2)]
        occ_ref[q // 2] = jnp.concatenate(two, 0).astype(BF16)


def pick_occupied(first, got, after):
    return pl.pallas_call(
        pick_occupied_kernel,
        out_shape=jax.ShapeDtypeStruct((8, 16, 128), BF16),
        in_specs=[
            pl.BlockSpec(memory_space=SMEM),
            pl.BlockSpec(memory_space=VMEM),
            pl.BlockSpec(memory_space=pl.ANY),
        ],
        out_specs=pl.BlockSpec(memory_space=VMEM),
        name="pick_occupied",
    )(first, got, after)


CAME_BY = ((0, 4), (7, 3), (1, 5), (6, 2))


def deal_kernel(z_ref, *refs):
    got_refs, (out_ref, held) = refs[:4], refs[4:]
    for got_ref, steps in zip(got_refs, CAME_BY):
        for n in range(2):
            held[steps[n]] = got_ref[n].astype(F32)
    for g in range(2):
        for m in range(0, 4, 2):
            sources = [(4 * g + m + n - z_ref[0] + 8) % 8 for n in range(2)]
            for q in range(16):
                spot = 8 * (q % 2)
                rows = jnp.concatenate([held[s, q // 2, spot : spot + 8] for s in sources], 0)
                out_ref[2 * q + g, 8 * m : 8 * m + 16] = rows.astype(BF16)


def deal(z, got):
    return pl.pallas_call(
        deal_kernel,
        out_shape=jax.ShapeDtypeStruct((32, 32, 128), BF16),
        in_specs=[pl.BlockSpec(memory_space=SMEM)] + [pl.BlockSpec(memory_space=VMEM)] * 4,
        out_specs=pl.BlockSpec(memory_space=VMEM),
        scratch_shapes=[pltpu.VMEM((8, 8, 16, 128), F32)],
        name="deal",
    )(z, *got)


def weight_kernel(half_ref, column_ref, occ_ref, spread_ref, cos_ref, sin_ref, out_ref):
    half = half_ref[0]

    def step(yp, carry):
        piece, odd = yp // 2, yp % 2
        occ = jnp.concatenate([occ_ref[2 * piece + half], occ_ref[2 * piece + 1 - half]], 0)
        wide = lax.dot_general(occ, spread_ref[odd], (((0,), (0,)), ((), ())), preferred_element_type=F32)
        for g in range(2):
            ac, as_ = cos_ref[g], sin_ref[g]
            for u in range(2):
                c, s = column_ref[0, 32 * u + yp], column_ref[1, 32 * u + yp]
                tr = ac * c - as_ * s
                ti = as_ * c + ac * s
                real = wide[32 * u : 32 * u + 32, 128 * g : 128 * g + 128]
                imag = wide[64 + 32 * u : 96 + 32 * u, 128 * g : 128 * g + 128]
                wr = (real * tr + imag * ti).astype(BF16)
                wi = real * ti - imag * tr
                base = 128 * g + 32 * u
                out_ref[yp, base : base + 32, :128] = wr
                out_ref[yp, base : base + 32, 128:] = wi.astype(BF16)
                out_ref[yp, base + 64 : base + 96, :128] = (-wi).astype(BF16)
                out_ref[yp, base + 64 : base + 96, 128:] = wr
        return carry

    lax.fori_loop(0, 32, step, 0, unroll=8)


def weights_of(half, column, occ, spread, cosine, sine_part):
    return pl.pallas_call(
        weight_kernel,
        out_shape=jax.ShapeDtypeStruct((32, 256, 256), BF16),
        in_specs=[pl.BlockSpec(memory_space=SMEM)] * 2 + [pl.BlockSpec(memory_space=VMEM)] * 4,
        out_specs=pl.BlockSpec(memory_space=VMEM),
        compiler_params=pltpu.CompilerParams(vmem_limit_bytes=24 << 20),
        cost_estimate=pl.CostEstimate(flops=32 * 2 * 128 * 32 * 256, bytes_accessed=6 << 20, transcendentals=0),
        name="weights",
    )(half, column, occ, spread, cosine, sine_part)


def chunk_kernel(parts, place_ref, *refs):
    vir_refs, (weight_ref, row_ref, scale_ref, _, out_ref, total, ready, sems) = refs[:-8], refs[-8:]
    lane = lax.broadcasted_iota(jnp.int32, (32, 256), 1)
    upper = (lane // 32) % 2 == 0
    copies = []
    for n, part in enumerate(parts):
        here = vir_refs[: 2 * part]
        vir_refs = vir_refs[2 * part :]
        yp = 0
        for own_ref, other_ref in zip(here[0::2], here[1::2]):
            for step in range(own_ref.shape[0]):
                both = jnp.concatenate([own_ref[step], other_ref[step]], 1)
                nought = jnp.zeros_like(both)
                split = jnp.concatenate([jnp.where(upper, both, nought), jnp.where(upper, nought, both)], 0)
                sums = jnp.dot(split, weight_ref[yp], preferred_element_type=F32)
                for u in range(2):
                    for c in range(2):
                        block = sums[32 * u : 32 * u + 32, 128 * c : 128 * c + 128]
                        total[n, c, pl.ds(32 * u + yp, 32, stride=PITCH), :] = block
                yp += 1

        for a in range(32):
            left = jnp.concatenate([total[n, c, PITCH * a : PITCH * a + 64, :] for c in range(2)], 0).astype(BF16)
            result = lax.dot_general(left, row_ref[...], (((0,), (0,)), ((), ())), preferred_element_type=F32)
            ready[n, :, a] = (result.reshape(16, 8, 128) * scale_ref[...][None]).astype(BF16)
            if a % 8 == 7:
                copy = pltpu.make_async_copy(
                    ready.at[n, :, pl.ds(a - 7, 8)],
                    out_ref.at[:, pl.ds(32 * place_ref[n] + (a - 7), 8)],
                    sems.at[n, a // 8],
                )
                copy.start()
                copies.append(copy)
    for copy in copies:
        copy.wait()


def chunk(places, virs, weights, row_table, scale, out):
    n = len(virs)
    args = [v for vir in virs for v in vir] + [weights, row_table, scale]
    return pl.pallas_call(
        functools.partial(chunk_kernel, [len(vir) // 2 for vir in virs]),
        out_shape=jax.ShapeDtypeStruct(out.shape, BF16),
        in_specs=[pl.BlockSpec(memory_space=SMEM)]
        + [pl.BlockSpec(memory_space=VMEM)] * len(args)
        + [pl.BlockSpec(memory_space=pl.ANY)],
        out_specs=pl.BlockSpec(memory_space=pl.ANY),
        scratch_shapes=[
            pltpu.VMEM((n, 2, 32 * PITCH, 128), F32),
            pltpu.VMEM((n, 16, 32, 8, 128), BF16),
            pltpu.SemaphoreType.DMA((n, 4)),
        ],
        input_output_aliases={len(args) + 1: 0},
        compiler_params=pltpu.CompilerParams(vmem_limit_bytes=24 << 20),
        cost_estimate=pl.CostEstimate(flops=n << 31, bytes_accessed=n << 20, transcendentals=0),
        name="chunk",
    )(jnp.stack(places), *args, out)


def empty_kernel(out_ref):
    pass


def empty(shape):
    return pl.pallas_call(
        empty_kernel,
        out_shape=jax.ShapeDtypeStruct(shape, BF16),
        out_specs=pl.BlockSpec(memory_space=pl.ANY),
        name="empty",
    )()


def spread_table():
    table = np.zeros((2, 2, 4, 2, 4, 2, 16, 8), np.float32)
    for u in range(2):
        for g in range(2):
            for m in range(4):
                for o in range(4):
                    table[u, g, m, u, o, g, 4 * m + o, :] = 1.0
    return jnp.asarray(table.reshape(2, 64, 256), BF16)


def on_device(occupied, virtual, coulomb, transfer_pairs, shifts):
    points = 64
    z, half = lax.axis_index("kp"), lax.axis_index("ga")
    got = lax.all_to_all(open_up(transfer_pairs, virtual[0], occupied[0]), "ka", 0, 0, tiled=False)
    first, second = got[:, 72, 0].astype(jnp.int32), got[:, 73, 0].astype(jnp.int32)
    picked = pick_virtual(second, got)
    occ = pick_occupied(first, got, picked)
    own = lax.all_to_all(picked, "ka", 0, 0, tiled=False).reshape(32, 32, 128)
    two = jnp.stack([occ, lax.ppermute(occ, "kp", [(i, (i + 4) % 8) for i in range(8)])])
    occ = [two] + [lax.ppermute(two, "kp", [(i, (i + s) % 8) for i in range(8)]) for s in (1, -1, 2)]
    occ = lax.all_to_all(deal(z.reshape(1), occ), ("ka", "ga"), 0, 0, tiled=False)

    grid = jnp.arange(points, dtype=jnp.int32)
    cosine, sine_part = phase_angle_parts(points)
    planes = 8 * z + jnp.arange(8, dtype=jnp.int32)
    col_cos = jnp.take(cosine, planes, axis=0).astype(BF16).astype(F32).T
    col_sin = jnp.take(sine_part, planes, axis=0).astype(BF16).astype(F32).T
    turn_x = ((shifts[0, 0] * grid) % points).astype(F32) * (2.0 * math.pi / points)
    turn_y = ((shifts[0, 1] * grid) % points).astype(F32) * (2.0 * math.pi / points)
    cx, sx = jnp.cos(turn_x)[:, None], -jnp.sin(turn_x)[:, None]
    tab_cos = jnp.tile(col_cos * cx + col_sin * sx, (1, 16)).reshape(2, 32, 128)
    tab_sin = jnp.tile(col_cos * sx - col_sin * cx, (1, 16)).reshape(2, 32, 128)
    column = jnp.stack([jnp.cos(turn_y), -jnp.sin(turn_y)])
    scale = lax.dynamic_slice_in_dim(coulomb[0], 8 * z, 8, 0)
    scale = jnp.concatenate([scale, scale], 1) * (1.0 / points)
    row_table = row_table_of(points)

    forward = [(i, (i + 1) % 8) for i in range(8)]
    backward = [(i, (i - 1) % 8) for i in range(8)]
    tab_cos = jnp.where(half == 0, tab_cos, tab_cos[::-1])
    tab_sin = jnp.where(half == 0, tab_sin, tab_sin[::-1])
    weights = weights_of(half.reshape(1), column, occ, spread_table(), tab_cos, tab_sin)

    def add(shifted, virs, out):
        return chunk([(z - s) % 8 for s in shifted], virs, weights, row_table, scale, out)

    other = lax.ppermute(own, "ga", [(0, 1), (1, 0)])
    out = add([0], [[own, other]], empty((16, 256, 8, 128)))
    ahead = behind = [own, other]
    for s in range(1, 4):
        ahead = [lax.ppermute(v, "kp", forward) for v in ahead]
        behind = [lax.ppermute(v, "kp", backward) for v in behind]
        out = add([s, -s], [ahead, behind], out)
    lower = [lax.ppermute(v[:16], "kp", forward) for v in ahead]
    higher = [lax.ppermute(v[16:], "kp", backward) for v in behind]
    out = add([4], [lower + higher], out)
    return out[None]


def solution(mesh):
    in_specs = (
        P("ka", "kp", "ga", None),
        P("ka", "kp", "ga", None),
        P("ka", None, None),
        P("ka", None),
        P("ka", None),
    )
    out_specs = P("ka", "ga", None, "kp", None)
    return jax.shard_map(
        on_device, mesh=mesh, in_specs=in_specs, out_specs=out_specs, check_vma=False
    )
```

```python
import functools
import math

import jax
import jax.numpy as jnp
import numpy as np
from jax import lax
from jax.experimental import pallas as pl
from jax.experimental.pallas import tpu as pltpu
from jax.sharding import PartitionSpec as P

F32 = jnp.float32
PITCH = 72
BF16 = jnp.bfloat16
VMEM = pltpu.VMEM
SMEM = pltpu.SMEM


def phase_angle_parts(points):
    index = jnp.arange(points, dtype=jnp.int32)
    windings = index[:, None] * index[None, :] % points
    angles = windings.astype(F32) * (2.0 * math.pi / points)
    return (jnp.cos(angles), jnp.sin(angles))


def row_table_of(points):
    cosine, sine_part = phase_angle_parts(points)
    upper_rows = jnp.concatenate([cosine, -sine_part], 1)
    lower_rows = jnp.concatenate([sine_part, cosine], 1)
    return jnp.concatenate([upper_rows, lower_rows], 0).astype(BF16)


def turn_orbitals(orb_ref, spread):
    norb = orb_ref.shape[0]
    pitch = spread.shape[0] // 32
    for g in range(norb // 4):
        turned = orb_ref[4 * g : 4 * g + 4].reshape(128, 128).astype(F32).T
        for o in range(4):
            lanes = [turned[32 * t : 32 * t + 32, 32 * o : 32 * o + 32] for t in range(4)]
            spread[pl.ds(4 * g + o, 32, stride=pitch), :] = jnp.concatenate(lanes, 1)
    rows = [spread[pitch * yp : pitch * yp + norb] for yp in range(32)]
    return jnp.concatenate(rows, 0).reshape(16, 2 * norb, 128)


def open_kernel(pairs_ref, vir_ref, occ_ref, out_ref, spread, spread_occ):
    out_ref[:, :64] = turn_orbitals(vir_ref, spread).astype(BF16)
    row = lax.broadcasted_iota(jnp.int32, (16, 8, 128), 1)
    told = jnp.where(row == 0, pairs_ref[0, 0], jnp.where(row == 1, pairs_ref[0, 1], 0))
    rest = [turn_orbitals(occ_ref, spread_occ), told.astype(F32)]
    out_ref[:, 64:] = jnp.concatenate(rest, 1).astype(BF16)


def open_up(pairs, virtual, occupied):
    return pl.pallas_call(
        open_kernel,
        out_shape=jax.ShapeDtypeStruct((16, 80, 128), BF16),
        in_specs=[pl.BlockSpec(memory_space=SMEM)] + [pl.BlockSpec(memory_space=VMEM)] * 2,
        out_specs=pl.BlockSpec(memory_space=VMEM),
        scratch_shapes=[pltpu.VMEM((32 * 40, 128), F32), pltpu.VMEM((32 * 8, 128), F32)],
        name="open_up",
    )(pairs, virtual, occupied)


def pick_virtual_kernel(second_ref, got_ref, vir_ref):
    for q in range(16):
        for g in range(2):
            vir_ref[2 * q + g] = got_ref[second_ref[q], :64]


def pick_virtual(second, got):
    return pl.pallas_call(
        pick_virtual_kernel,
        out_shape=jax.ShapeDtypeStruct((32, 64, 128), BF16),
        in_specs=[pl.BlockSpec(memory_space=SMEM), pl.BlockSpec(memory_space=VMEM)],
        out_specs=pl.BlockSpec(memory_space=VMEM),
        name="pick_virtual",
    )(second, got)


def pick_occupied_kernel(first_ref, got_ref, _, occ_ref):
    for q in range(0, 16, 2):
        two = [got_ref[first_ref[q + n], 64:].astype(F32)[:8] for n in range(2)]
        occ_ref[q // 2] = jnp.concatenate(two, 0).astype(BF16)


def pick_occupied(first, got, after):
    return pl.pallas_call(
        pick_occupied_kernel,
        out_shape=jax.ShapeDtypeStruct((8, 16, 128), BF16),
        in_specs=[
            pl.BlockSpec(memory_space=SMEM),
            pl.BlockSpec(memory_space=VMEM),
            pl.BlockSpec(memory_space=pl.ANY),
        ],
        out_specs=pl.BlockSpec(memory_space=VMEM),
        name="pick_occupied",
    )(first, got, after)


CAME_BY = ((0, 4), (7, 3), (1, 5), (6, 2))


def deal_kernel(z_ref, *refs):
    got_refs, (out_ref, held) = refs[:4], refs[4:]
    for got_ref, steps in zip(got_refs, CAME_BY):
        for n in range(2):
            held[steps[n]] = got_ref[n].astype(F32)
    for g in range(2):
        for m in range(0, 4, 2):
            sources = [(4 * g + m + n - z_ref[0] + 8) % 8 for n in range(2)]
            for q in range(16):
                spot = 8 * (q % 2)
                rows = jnp.concatenate([held[s, q // 2, spot : spot + 8] for s in sources], 0)
                out_ref[2 * q + g, 8 * m : 8 * m + 16] = rows.astype(BF16)


def deal(z, got):
    return pl.pallas_call(
        deal_kernel,
        out_shape=jax.ShapeDtypeStruct((32, 32, 128), BF16),
        in_specs=[pl.BlockSpec(memory_space=SMEM)] + [pl.BlockSpec(memory_space=VMEM)] * 4,
        out_specs=pl.BlockSpec(memory_space=VMEM),
        scratch_shapes=[pltpu.VMEM((8, 8, 16, 128), F32)],
        name="deal",
    )(z, *got)


def weight_kernel(column_ref, occ_ref, spread_ref, cos_ref, sin_ref, out_ref):
    def step(yp, carry):
        piece, odd = yp // 2, yp % 2
        occ = jnp.concatenate([occ_ref[2 * piece], occ_ref[2 * piece + 1]], 0)
        wide = lax.dot_general(occ, spread_ref[odd], (((0,), (0,)), ((), ())), preferred_element_type=F32)
        for g in range(2):
            ac, as_ = cos_ref[g], sin_ref[g]
            for u in range(2):
                c, s = column_ref[0, 32 * u + yp], column_ref[1, 32 * u + yp]
                tr = ac * c - as_ * s
                ti = as_ * c + ac * s
                real = wide[32 * u : 32 * u + 32, 128 * g : 128 * g + 128]
                imag = wide[64 + 32 * u : 96 + 32 * u, 128 * g : 128 * g + 128]
                wr = (real * tr + imag * ti).astype(BF16)
                wi = real * ti - imag * tr
                base = 128 * g + 32 * u
                out_ref[yp, base : base + 32, :128] = wr
                out_ref[yp, base : base + 32, 128:] = wi.astype(BF16)
                out_ref[yp, base + 64 : base + 96, :128] = (-wi).astype(BF16)
                out_ref[yp, base + 64 : base + 96, 128:] = wr
        return carry

    lax.fori_loop(0, 32, step, 0, unroll=8)


def weights_of(column, occ, spread, cosine, sine_part):
    return pl.pallas_call(
        weight_kernel,
        out_shape=jax.ShapeDtypeStruct((32, 256, 256), BF16),
        in_specs=[pl.BlockSpec(memory_space=SMEM)] + [pl.BlockSpec(memory_space=VMEM)] * 4,
        out_specs=pl.BlockSpec(memory_space=VMEM),
        compiler_params=pltpu.CompilerParams(vmem_limit_bytes=24 << 20),
        cost_estimate=pl.CostEstimate(flops=32 * 2 * 128 * 32 * 256, bytes_accessed=6 << 20, transcendentals=0),
        name="weights",
    )(column, occ, spread, cosine, sine_part)


def chunk_kernel(parts, place_ref, *refs):
    vir_refs, (weight_ref, row_ref, scale_ref, _, out_ref, total, ready, sems) = refs[:-8], refs[-8:]
    lane = lax.broadcasted_iota(jnp.int32, (32, 256), 1)
    upper = (lane // 32) % 2 == 0
    copies = []
    for n, part in enumerate(parts):
        here = vir_refs[:part]
        vir_refs = vir_refs[part:]
        yp = 0
        for vir_ref in here:
            for step in range(vir_ref.shape[0]):
                rows = slice(32 * (step % 2), 32 * (step % 2) + 32)
                both = [vir_ref[step // 2 * 2 + g, rows] for g in range(2)]
                both = jnp.concatenate(both, 1)
                nought = jnp.zeros_like(both)
                split = jnp.concatenate([jnp.where(upper, both, nought), jnp.where(upper, nought, both)], 0)
                sums = jnp.dot(split, weight_ref[yp], preferred_element_type=F32)
                for u in range(2):
                    for c in range(2):
                        block = sums[32 * u : 32 * u + 32, 128 * c : 128 * c + 128]
                        total[n, c, pl.ds(32 * u + yp, 32, stride=PITCH), :] = block
                yp += 1

        for a in range(32):
            left = jnp.concatenate([total[n, c, PITCH * a : PITCH * a + 64, :] for c in range(2)], 0).astype(BF16)
            result = lax.dot_general(left, row_ref[...], (((0,), (0,)), ((), ())), preferred_element_type=F32)
            ready[n, :, a] = (result.reshape(16, 8, 128) * scale_ref[...][None]).astype(BF16)
            if a % 8 == 7:
                copy = pltpu.make_async_copy(
                    ready.at[n, :, pl.ds(a - 7, 8)],
                    out_ref.at[:, pl.ds(32 * place_ref[n] + (a - 7), 8)],
                    sems.at[n, a // 8],
                )
                copy.start()
                copies.append(copy)
    for copy in copies:
        copy.wait()


def chunk(places, virs, weights, row_table, scale, out):
    n = len(virs)
    args = [v for vir in virs for v in vir] + [weights, row_table, scale]
    return pl.pallas_call(
        functools.partial(chunk_kernel, [len(vir) for vir in virs]),
        out_shape=jax.ShapeDtypeStruct(out.shape, BF16),
        in_specs=[pl.BlockSpec(memory_space=SMEM)]
        + [pl.BlockSpec(memory_space=VMEM)] * len(args)
        + [pl.BlockSpec(memory_space=pl.ANY)],
        out_specs=pl.BlockSpec(memory_space=pl.ANY),
        scratch_shapes=[
            pltpu.VMEM((n, 2, 32 * PITCH, 128), F32),
            pltpu.VMEM((n, 16, 32, 8, 128), BF16),
            pltpu.SemaphoreType.DMA((n, 4)),
        ],
        input_output_aliases={len(args) + 1: 0},
        compiler_params=pltpu.CompilerParams(vmem_limit_bytes=24 << 20),
        cost_estimate=pl.CostEstimate(flops=n << 31, bytes_accessed=n << 20, transcendentals=0),
        name="chunk",
    )(jnp.stack(places), *args, out)


def empty_kernel(out_ref):
    pass


def empty(shape):
    return pl.pallas_call(
        empty_kernel,
        out_shape=jax.ShapeDtypeStruct(shape, BF16),
        out_specs=pl.BlockSpec(memory_space=pl.ANY),
        name="empty",
    )()


def spread_table():
    table = np.zeros((2, 2, 4, 2, 4, 2, 16, 8), np.float32)
    for u in range(2):
        for g in range(2):
            for m in range(4):
                for o in range(4):
                    table[u, g, m, u, o, g, 4 * m + o, :] = 1.0
    return jnp.asarray(table.reshape(2, 64, 256), BF16)


def on_device(occupied, virtual, coulomb, transfer_pairs, shifts):
    points = 64
    z = lax.axis_index("kp")
    got = lax.all_to_all(open_up(transfer_pairs, virtual[0], occupied[0]), "ka", 0, 0, tiled=False)
    first, second = got[:, 72, 0].astype(jnp.int32), got[:, 73, 0].astype(jnp.int32)
    picked = pick_virtual(second, got)
    occ = pick_occupied(first, got, picked)
    vir = lax.all_to_all(picked, ("ka", "ga"), 0, 0, tiled=False)
    two = jnp.stack([occ, lax.ppermute(occ, "kp", [(i, (i + 4) % 8) for i in range(8)])])
    occ = [two] + [lax.ppermute(two, "kp", [(i, (i + s) % 8) for i in range(8)]) for s in (1, -1, 2)]
    occ = lax.all_to_all(deal(z.reshape(1), occ), ("ka", "ga"), 0, 0, tiled=False)

    grid = jnp.arange(points, dtype=jnp.int32)
    cosine, sine_part = phase_angle_parts(points)
    planes = 8 * z + jnp.arange(8, dtype=jnp.int32)
    col_cos = jnp.take(cosine, planes, axis=0).astype(BF16).astype(F32).T
    col_sin = jnp.take(sine_part, planes, axis=0).astype(BF16).astype(F32).T
    turn_x = ((shifts[0, 0] * grid) % points).astype(F32) * (2.0 * math.pi / points)
    turn_y = ((shifts[0, 1] * grid) % points).astype(F32) * (2.0 * math.pi / points)
    cx, sx = jnp.cos(turn_x)[:, None], -jnp.sin(turn_x)[:, None]
    tab_cos = jnp.tile(col_cos * cx + col_sin * sx, (1, 16)).reshape(2, 32, 128)
    tab_sin = jnp.tile(col_cos * sx - col_sin * cx, (1, 16)).reshape(2, 32, 128)
    column = jnp.stack([jnp.cos(turn_y), -jnp.sin(turn_y)])
    scale = lax.dynamic_slice_in_dim(coulomb[0], 8 * z, 8, 0)
    scale = jnp.concatenate([scale, scale], 1) * (1.0 / points)
    row_table = row_table_of(points)

    forward = [(i, (i + 1) % 8) for i in range(8)]
    backward = [(i, (i - 1) % 8) for i in range(8)]
    weights = weights_of(column, occ, spread_table(), tab_cos, tab_sin)

    def add(shifted, virs, out):
        return chunk([(z - s) % 8 for s in shifted], virs, weights, row_table, scale, out)

    out = add([0], [[vir]], empty((16, 256, 8, 128)))
    ahead = behind = vir
    for s in range(1, 4):
        ahead = lax.ppermute(ahead, "kp", forward)
        behind = lax.ppermute(behind, "kp", backward)
        out = add([s, -s], [[ahead], [behind]], out)
    lower = lax.ppermute(ahead[:16], "kp", forward)
    higher = lax.ppermute(behind[16:], "kp", backward)
    out = add([4], [[lower, higher]], out)
    return out[None]


def solution(mesh):
    in_specs = (
        P("ka", "kp", "ga", None),
        P("ka", "kp", "ga", None),
        P("ka", None, None),
        P("ka", None),
        P("ka", None),
    )
    out_specs = P("ka", "ga", None, "kp", None)
    return jax.shard_map(
        on_device, mesh=mesh, in_specs=in_specs, out_specs=out_specs, check_vma=False
    )
```

```python
import functools
import math

import jax
import jax.numpy as jnp
import numpy as np
from jax import lax
from jax.experimental import pallas as pl
from jax.experimental.pallas import tpu as pltpu
from jax.sharding import PartitionSpec as P

F32 = jnp.float32
PITCH = 72
BF16 = jnp.bfloat16
VMEM = pltpu.VMEM
SMEM = pltpu.SMEM


def phase_angle_parts(points):
    index = jnp.arange(points, dtype=jnp.int32)
    windings = index[:, None] * index[None, :] % points
    angles = windings.astype(F32) * (2.0 * math.pi / points)
    return (jnp.cos(angles), jnp.sin(angles))


def row_table_of(points):
    cosine, sine_part = phase_angle_parts(points)
    upper_rows = jnp.concatenate([cosine, -sine_part], 1)
    lower_rows = jnp.concatenate([sine_part, cosine], 1)
    return jnp.concatenate([upper_rows, lower_rows], 0).astype(BF16)


def turn_orbitals(orb_ref, spread):
    norb = orb_ref.shape[0]
    pitch = spread.shape[0] // 32
    for g in range(norb // 4):
        turned = orb_ref[4 * g : 4 * g + 4].reshape(128, 128).astype(F32).T
        for o in range(4):
            lanes = [turned[32 * t : 32 * t + 32, 32 * o : 32 * o + 32] for t in range(4)]
            spread[pl.ds(4 * g + o, 32, stride=pitch), :] = jnp.concatenate(lanes, 1)
    rows = [spread[pitch * yp : pitch * yp + norb] for yp in range(32)]
    return jnp.concatenate(rows, 0).reshape(16, 2 * norb, 128)


def open_kernel(pairs_ref, vir_ref, occ_ref, out_ref, spread, spread_occ):
    out_ref[:, :64] = turn_orbitals(vir_ref, spread).astype(BF16)
    row = lax.broadcasted_iota(jnp.int32, (16, 8, 128), 1)
    told = jnp.where(row == 0, pairs_ref[0, 0], jnp.where(row == 1, pairs_ref[0, 1], 0))
    rest = [turn_orbitals(occ_ref, spread_occ), told.astype(F32)]
    out_ref[:, 64:] = jnp.concatenate(rest, 1).astype(BF16)


def open_up(pairs, virtual, occupied):
    return pl.pallas_call(
        open_kernel,
        out_shape=jax.ShapeDtypeStruct((16, 80, 128), BF16),
        in_specs=[pl.BlockSpec(memory_space=SMEM)] + [pl.BlockSpec(memory_space=VMEM)] * 2,
        out_specs=pl.BlockSpec(memory_space=VMEM),
        scratch_shapes=[pltpu.VMEM((32 * 40, 128), F32), pltpu.VMEM((32 * 8, 128), F32)],
        name="open_up",
    )(pairs, virtual, occupied)


def told_points(got_ref, column):
    return [got_ref[q, 64:].astype(F32).astype(jnp.int32)[8 + column, 0] for q in range(16)]


def pick_virtual_kernel(got_ref, vir_ref):
    second = told_points(got_ref, 1)
    for q in range(16):
        for g in range(2):
            vir_ref[2 * q + g] = got_ref[second[q], :64]


def pick_virtual(got):
    return pl.pallas_call(
        pick_virtual_kernel,
        out_shape=jax.ShapeDtypeStruct((32, 64, 128), BF16),
        in_specs=[pl.BlockSpec(memory_space=VMEM)],
        out_specs=pl.BlockSpec(memory_space=VMEM),
        name="pick_virtual",
    )(got)


def pick_occupied_kernel(got_ref, _, occ_ref):
    first = told_points(got_ref, 0)
    for q in range(0, 16, 2):
        two = [got_ref[first[q + n], 64:].astype(F32)[:8] for n in range(2)]
        occ_ref[q // 2] = jnp.concatenate(two, 0).astype(BF16)


def pick_occupied(got, after):
    return pl.pallas_call(
        pick_occupied_kernel,
        out_shape=jax.ShapeDtypeStruct((8, 16, 128), BF16),
        in_specs=[pl.BlockSpec(memory_space=VMEM), pl.BlockSpec(memory_space=pl.ANY)],
        out_specs=pl.BlockSpec(memory_space=VMEM),
        name="pick_occupied",
    )(got, after)


CAME_BY = ((0, 7, 1), (5, 4, 6), (3, 2, 4))


def deal_kernel(z_ref, *refs):
    got_refs, (out_ref, held) = refs[:3], refs[3:]
    for got_ref, steps in zip(got_refs, CAME_BY):
        for n in range(3):
            held[steps[n]] = got_ref[n].astype(F32)
    for g in range(2):
        for m in range(0, 4, 2):
            sources = [(4 * g + m + n - z_ref[0] + 8) % 8 for n in range(2)]
            for q in range(16):
                spot = 8 * (q % 2)
                rows = jnp.concatenate([held[s, q // 2, spot : spot + 8] for s in sources], 0)
                out_ref[2 * q + g, 8 * m : 8 * m + 16] = rows.astype(BF16)


def deal(z, got):
    return pl.pallas_call(
        deal_kernel,
        out_shape=jax.ShapeDtypeStruct((32, 32, 128), BF16),
        in_specs=[pl.BlockSpec(memory_space=SMEM)] + [pl.BlockSpec(memory_space=VMEM)] * 3,
        out_specs=pl.BlockSpec(memory_space=VMEM),
        scratch_shapes=[pltpu.VMEM((8, 8, 16, 128), F32)],
        name="deal",
    )(z, *got)


def weight_kernel(column_ref, occ_ref, spread_ref, cos_ref, sin_ref, out_ref):
    def step(yp, carry):
        piece, odd = yp // 2, yp % 2
        occ = jnp.concatenate([occ_ref[2 * piece], occ_ref[2 * piece + 1]], 0)
        wide = lax.dot_general(occ, spread_ref[odd], (((0,), (0,)), ((), ())), preferred_element_type=F32)
        for g in range(2):
            ac, as_ = cos_ref[g], sin_ref[g]
            for u in range(2):
                c, s = column_ref[0, 32 * u + yp], column_ref[1, 32 * u + yp]
                tr = ac * c - as_ * s
                ti = as_ * c + ac * s
                real = wide[32 * u : 32 * u + 32, 128 * g : 128 * g + 128]
                imag = wide[64 + 32 * u : 96 + 32 * u, 128 * g : 128 * g + 128]
                wr = (real * tr + imag * ti).astype(BF16)
                wi = real * ti - imag * tr
                base = 128 * g + 32 * u
                out_ref[yp, base : base + 32, :128] = wr
                out_ref[yp, base : base + 32, 128:] = wi.astype(BF16)
                out_ref[yp, base + 64 : base + 96, :128] = (-wi).astype(BF16)
                out_ref[yp, base + 64 : base + 96, 128:] = wr
        return carry

    lax.fori_loop(0, 32, step, 0, unroll=8)


def weights_of(column, occ, spread, cosine, sine_part):
    return pl.pallas_call(
        weight_kernel,
        out_shape=jax.ShapeDtypeStruct((32, 256, 256), BF16),
        in_specs=[pl.BlockSpec(memory_space=SMEM)] + [pl.BlockSpec(memory_space=VMEM)] * 4,
        out_specs=pl.BlockSpec(memory_space=VMEM),
        compiler_params=pltpu.CompilerParams(vmem_limit_bytes=24 << 20),
        cost_estimate=pl.CostEstimate(flops=32 * 2 * 128 * 32 * 256, bytes_accessed=6 << 20, transcendentals=0),
        name="weights",
    )(column, occ, spread, cosine, sine_part)


def chunk_kernel(parts, place_ref, *refs):
    vir_refs, (weight_ref, row_ref, scale_ref, _, out_ref, total, ready, sems) = refs[:-8], refs[-8:]
    lane = lax.broadcasted_iota(jnp.int32, (32, 256), 1)
    upper = (lane // 32) % 2 == 0
    copies = []
    for n, part in enumerate(parts):
        here = vir_refs[:part]
        vir_refs = vir_refs[part:]
        yp = 0
        for vir_ref in here:
            for step in range(vir_ref.shape[0]):
                rows = slice(32 * (step % 2), 32 * (step % 2) + 32)
                both = [vir_ref[step // 2 * 2 + g, rows] for g in range(2)]
                both = jnp.concatenate(both, 1)
                nought = jnp.zeros_like(both)
                split = jnp.concatenate([jnp.where(upper, both, nought), jnp.where(upper, nought, both)], 0)
                sums = jnp.dot(split, weight_ref[yp], preferred_element_type=F32)
                for u in range(2):
                    for c in range(2):
                        block = sums[32 * u : 32 * u + 32, 128 * c : 128 * c + 128]
                        total[n, c, pl.ds(32 * u + yp, 32, stride=PITCH), :] = block
                yp += 1

        for a in range(32):
            left = jnp.concatenate([total[n, c, PITCH * a : PITCH * a + 64, :] for c in range(2)], 0).astype(BF16)
            result = lax.dot_general(left, row_ref[...], (((0,), (0,)), ((), ())), preferred_element_type=F32)
            ready[n, :, a] = (result.reshape(16, 8, 128) * scale_ref[...][None]).astype(BF16)
            if a % 8 == 7:
                copy = pltpu.make_async_copy(
                    ready.at[n, :, pl.ds(a - 7, 8)],
                    out_ref.at[:, pl.ds(32 * place_ref[n] + (a - 7), 8)],
                    sems.at[n, a // 8],
                )
                copy.start()
                copies.append(copy)
    for copy in copies:
        copy.wait()


def chunk(places, virs, weights, row_table, scale, out):
    n = len(virs)
    args = [v for vir in virs for v in vir] + [weights, row_table, scale]
    return pl.pallas_call(
        functools.partial(chunk_kernel, [len(vir) for vir in virs]),
        out_shape=jax.ShapeDtypeStruct(out.shape, BF16),
        in_specs=[pl.BlockSpec(memory_space=SMEM)]
        + [pl.BlockSpec(memory_space=VMEM)] * len(args)
        + [pl.BlockSpec(memory_space=pl.ANY)],
        out_specs=pl.BlockSpec(memory_space=pl.ANY),
        scratch_shapes=[
            pltpu.VMEM((n, 2, 32 * PITCH, 128), F32),
            pltpu.VMEM((n, 16, 32, 8, 128), BF16),
            pltpu.SemaphoreType.DMA((n, 4)),
        ],
        input_output_aliases={len(args) + 1: 0},
        compiler_params=pltpu.CompilerParams(vmem_limit_bytes=24 << 20),
        cost_estimate=pl.CostEstimate(flops=n << 31, bytes_accessed=n << 20, transcendentals=0),
        name="chunk",
    )(jnp.stack(places), *args, out)


def empty_kernel(out_ref):
    pass


def empty(shape):
    return pl.pallas_call(
        empty_kernel,
        out_shape=jax.ShapeDtypeStruct(shape, BF16),
        out_specs=pl.BlockSpec(memory_space=pl.ANY),
        name="empty",
    )()


def spread_table():
    table = np.zeros((2, 2, 4, 2, 4, 2, 16, 8), np.float32)
    for u in range(2):
        for g in range(2):
            for m in range(4):
                for o in range(4):
                    table[u, g, m, u, o, g, 4 * m + o, :] = 1.0
    return jnp.asarray(table.reshape(2, 64, 256), BF16)


def on_device(occupied, virtual, coulomb, transfer_pairs, shifts):
    points = 64
    z = lax.axis_index("kp")
    got = lax.all_to_all(open_up(transfer_pairs, virtual[0], occupied[0]), "ka", 0, 0, tiled=False)
    picked = pick_virtual(got)
    occ = pick_occupied(got, picked)
    vir = lax.all_to_all(picked, ("ka", "ga"), 0, 0, tiled=False)

    def shifted(block, s):
        return lax.ppermute(block, "kp", [(i, (i + s) % 8) for i in range(8)])

    near = jnp.stack([occ, shifted(occ, 1), shifted(occ, -1)])
    vir, *occ = lax.optimization_barrier((vir, near, shifted(near, 3), shifted(near, -3)))
    occ = lax.all_to_all(deal(z.reshape(1), occ), ("ka", "ga"), 0, 0, tiled=False)

    grid = jnp.arange(points, dtype=jnp.int32)
    cosine, sine_part = phase_angle_parts(points)
    planes = 8 * z + jnp.arange(8, dtype=jnp.int32)
    col_cos = jnp.take(cosine, planes, axis=0).astype(BF16).astype(F32).T
    col_sin = jnp.take(sine_part, planes, axis=0).astype(BF16).astype(F32).T
    turn_x = ((shifts[0, 0] * grid) % points).astype(F32) * (2.0 * math.pi / points)
    turn_y = ((shifts[0, 1] * grid) % points).astype(F32) * (2.0 * math.pi / points)
    cx, sx = jnp.cos(turn_x)[:, None], -jnp.sin(turn_x)[:, None]
    tab_cos = jnp.tile(col_cos * cx + col_sin * sx, (1, 16)).reshape(2, 32, 128)
    tab_sin = jnp.tile(col_cos * sx - col_sin * cx, (1, 16)).reshape(2, 32, 128)
    column = jnp.stack([jnp.cos(turn_y), -jnp.sin(turn_y)])
    scale = lax.dynamic_slice_in_dim(coulomb[0], 8 * z, 8, 0)
    scale = jnp.concatenate([scale, scale], 1) * (1.0 / points)
    row_table = row_table_of(points)

    forward = [(i, (i + 1) % 8) for i in range(8)]
    backward = [(i, (i - 1) % 8) for i in range(8)]
    weights = weights_of(column, occ, spread_table(), tab_cos, tab_sin)

    def add(shifted, virs, out):
        return chunk([(z - s) % 8 for s in shifted], virs, weights, row_table, scale, out)

    out = add([0], [[vir]], empty((16, 256, 8, 128)))
    ahead = behind = vir
    for s in range(1, 4):
        ahead = lax.ppermute(ahead, "kp", forward)
        behind = lax.ppermute(behind, "kp", backward)
        out = add([s, -s], [[ahead], [behind]], out)
    lower = lax.ppermute(ahead[:16], "kp", forward)
    higher = lax.ppermute(behind[16:], "kp", backward)
    out = add([4], [[lower, higher]], out)
    return out[None]


def solution(mesh):
    in_specs = (
        P("ka", "kp", "ga", None),
        P("ka", "kp", "ga", None),
        P("ka", None, None),
        P("ka", None),
        P("ka", None),
    )
    out_specs = P("ka", "ga", None, "kp", None)
    return jax.shard_map(
        on_device, mesh=mesh, in_specs=in_specs, out_specs=out_specs, check_vma=False
    )
```

```python
import functools
import math

import jax
import jax.numpy as jnp
import numpy as np
from jax import lax
from jax.experimental import pallas as pl
from jax.experimental.pallas import tpu as pltpu
from jax.sharding import PartitionSpec as P

F32 = jnp.float32
PITCH = 72
BF16 = jnp.bfloat16
VMEM = pltpu.VMEM
SMEM = pltpu.SMEM


def phase_angle_parts(points):
    index = jnp.arange(points, dtype=jnp.int32)
    windings = index[:, None] * index[None, :] % points
    angles = windings.astype(F32) * (2.0 * math.pi / points)
    return (jnp.cos(angles), jnp.sin(angles))


def row_table_of(points):
    cosine, sine_part = phase_angle_parts(points)
    upper_rows = jnp.concatenate([cosine, -sine_part], 1)
    lower_rows = jnp.concatenate([sine_part, cosine], 1)
    return jnp.concatenate([upper_rows, lower_rows], 0).astype(BF16)


def turn_orbitals(orb_ref, spread):
    norb = orb_ref.shape[0]
    pitch = spread.shape[0] // 32
    for g in range(norb // 4):
        turned = orb_ref[4 * g : 4 * g + 4].reshape(128, 128).astype(F32).T
        for o in range(4):
            lanes = [turned[32 * t : 32 * t + 32, 32 * o : 32 * o + 32] for t in range(4)]
            spread[pl.ds(4 * g + o, 32, stride=pitch), :] = jnp.concatenate(lanes, 1)
    rows = [spread[pitch * yp : pitch * yp + norb] for yp in range(32)]
    return jnp.concatenate(rows, 0).reshape(16, 2 * norb, 128)


def open_kernel(pairs_ref, vir_ref, occ_ref, out_ref, spread, spread_occ):
    out_ref[:, :64] = turn_orbitals(vir_ref, spread).astype(BF16)
    row = lax.broadcasted_iota(jnp.int32, (16, 8, 128), 1)
    told = jnp.where(row == 0, pairs_ref[0, 0], jnp.where(row == 1, pairs_ref[0, 1], 0))
    rest = [turn_orbitals(occ_ref, spread_occ), told.astype(F32)]
    out_ref[:, 64:] = jnp.concatenate(rest, 1).astype(BF16)


def open_up(pairs, virtual, occupied):
    return pl.pallas_call(
        open_kernel,
        out_shape=jax.ShapeDtypeStruct((16, 80, 128), BF16),
        in_specs=[pl.BlockSpec(memory_space=SMEM)] + [pl.BlockSpec(memory_space=VMEM)] * 2,
        out_specs=pl.BlockSpec(memory_space=VMEM),
        scratch_shapes=[pltpu.VMEM((32 * 40, 128), F32), pltpu.VMEM((32 * 8, 128), F32)],
        name="open_up",
    )(pairs, virtual, occupied)


def told_points(got_ref, column):
    return [got_ref[q, 64:].astype(F32).astype(jnp.int32)[8 + column, 0] for q in range(16)]


def pick_virtual_kernel(got_ref, vir_ref):
    second = told_points(got_ref, 1)
    for q in range(16):
        for g in range(2):
            vir_ref[2 * q + g] = got_ref[second[q], :64]


def pick_virtual(got):
    return pl.pallas_call(
        pick_virtual_kernel,
        out_shape=jax.ShapeDtypeStruct((32, 64, 128), BF16),
        in_specs=[pl.BlockSpec(memory_space=VMEM)],
        out_specs=pl.BlockSpec(memory_space=VMEM),
        name="pick_virtual",
    )(got)


def pick_occupied_kernel(got_ref, _, occ_ref):
    first = told_points(got_ref, 0)
    for q in range(0, 16, 2):
        two = [got_ref[first[q + n], 64:].astype(F32)[:8] for n in range(2)]
        occ_ref[q // 2] = jnp.concatenate(two, 0).astype(BF16)


def pick_occupied(got, after):
    return pl.pallas_call(
        pick_occupied_kernel,
        out_shape=jax.ShapeDtypeStruct((8, 16, 128), BF16),
        in_specs=[pl.BlockSpec(memory_space=VMEM), pl.BlockSpec(memory_space=pl.ANY)],
        out_specs=pl.BlockSpec(memory_space=VMEM),
        name="pick_occupied",
    )(got, after)


CAME_BY = ((0, 7, 1), (5, 4, 6), (3, 2, 4))


def deal_kernel(z_ref, *refs):
    got_refs, (out_ref, held) = refs[:3], refs[3:]
    for got_ref, steps in zip(got_refs, CAME_BY):
        for n in range(3):
            held[steps[n]] = got_ref[n].astype(F32)
    for g in range(2):
        for m in range(0, 4, 2):
            sources = [(4 * g + m + n - z_ref[0] + 8) % 8 for n in range(2)]
            for q in range(16):
                spot = 8 * (q % 2)
                rows = jnp.concatenate([held[s, q // 2, spot : spot + 8] for s in sources], 0)
                out_ref[2 * q + g, 8 * m : 8 * m + 16] = rows.astype(BF16)


def deal(z, got):
    return pl.pallas_call(
        deal_kernel,
        out_shape=jax.ShapeDtypeStruct((32, 32, 128), BF16),
        in_specs=[pl.BlockSpec(memory_space=SMEM)] + [pl.BlockSpec(memory_space=VMEM)] * 3,
        out_specs=pl.BlockSpec(memory_space=VMEM),
        scratch_shapes=[pltpu.VMEM((8, 8, 16, 128), F32)],
        name="deal",
    )(z, *got)


def weight_kernel(column_ref, occ_ref, spread_ref, cos_ref, sin_ref, out_ref):
    def step(yp, carry):
        piece, odd = yp // 2, yp % 2
        occ = jnp.concatenate([occ_ref[2 * piece], occ_ref[2 * piece + 1]], 0)
        wide = lax.dot_general(occ, spread_ref[odd], (((0,), (0,)), ((), ())), preferred_element_type=F32)
        for g in range(2):
            ac, as_ = cos_ref[g], sin_ref[g]
            for u in range(2):
                c, s = column_ref[0, 32 * u + yp], column_ref[1, 32 * u + yp]
                tr = ac * c - as_ * s
                ti = as_ * c + ac * s
                real = wide[32 * u : 32 * u + 32, 128 * g : 128 * g + 128]
                imag = wide[64 + 32 * u : 96 + 32 * u, 128 * g : 128 * g + 128]
                wr = (real * tr + imag * ti).astype(BF16)
                wi = real * ti - imag * tr
                base = 128 * g + 32 * u
                out_ref[yp, base : base + 32, :128] = wr
                out_ref[yp, base : base + 32, 128:] = wi.astype(BF16)
                out_ref[yp, base + 64 : base + 96, :128] = (-wi).astype(BF16)
                out_ref[yp, base + 64 : base + 96, 128:] = wr
        return carry

    lax.fori_loop(0, 32, step, 0, unroll=8)


def weights_of(column, occ, spread, cosine, sine_part):
    return pl.pallas_call(
        weight_kernel,
        out_shape=jax.ShapeDtypeStruct((32, 256, 256), BF16),
        in_specs=[pl.BlockSpec(memory_space=SMEM)] + [pl.BlockSpec(memory_space=VMEM)] * 4,
        out_specs=pl.BlockSpec(memory_space=VMEM),
        compiler_params=pltpu.CompilerParams(vmem_limit_bytes=24 << 20),
        cost_estimate=pl.CostEstimate(flops=32 * 2 * 128 * 32 * 256, bytes_accessed=6 << 20, transcendentals=0),
        name="weights",
    )(column, occ, spread, cosine, sine_part)


def chunk_kernel(parts, place_ref, *refs):
    vir_refs, (weight_ref, row_ref, scale_ref, _, out_ref, total, ready, sems) = refs[:-8], refs[-8:]
    lane = lax.broadcasted_iota(jnp.int32, (32, 256), 1)
    upper = (lane // 32) % 2 == 0
    copies = []
    for n, part in enumerate(parts):
        here = vir_refs[:part]
        vir_refs = vir_refs[part:]
        yp = 0
        for vir_ref in here:
            for step in range(vir_ref.shape[0]):
                rows = slice(32 * (step % 2), 32 * (step % 2) + 32)
                both = [vir_ref[step // 2 * 2 + g, rows] for g in range(2)]
                both = jnp.concatenate(both, 1)
                nought = jnp.zeros_like(both)
                split = jnp.concatenate([jnp.where(upper, both, nought), jnp.where(upper, nought, both)], 0)
                sums = jnp.dot(split, weight_ref[yp], preferred_element_type=F32)
                for u in range(2):
                    for c in range(2):
                        block = sums[32 * u : 32 * u + 32, 128 * c : 128 * c + 128]
                        total[n, c, pl.ds(32 * u + yp, 32, stride=PITCH), :] = block
                yp += 1

        for a in range(32):
            left = jnp.concatenate([total[n, c, PITCH * a : PITCH * a + 64, :] for c in range(2)], 0).astype(BF16)
            result = lax.dot_general(left, row_ref[...], (((0,), (0,)), ((), ())), preferred_element_type=F32)
            ready[n, :, a] = (result.reshape(16, 8, 128) * scale_ref[...][None]).astype(BF16)
            if a % 8 == 7:
                copy = pltpu.make_async_copy(
                    ready.at[n, :, pl.ds(a - 7, 8)],
                    out_ref.at[:, pl.ds(32 * place_ref[n] + (a - 7), 8)],
                    sems.at[n, a // 8],
                )
                copy.start()
                copies.append(copy)
    for copy in copies:
        copy.wait()


def chunk(places, virs, weights, row_table, scale, out):
    n = len(virs)
    args = [v for vir in virs for v in vir] + [weights, row_table, scale]
    return pl.pallas_call(
        functools.partial(chunk_kernel, [len(vir) for vir in virs]),
        out_shape=jax.ShapeDtypeStruct(out.shape, BF16),
        in_specs=[pl.BlockSpec(memory_space=SMEM)]
        + [pl.BlockSpec(memory_space=VMEM)] * len(args)
        + [pl.BlockSpec(memory_space=pl.ANY)],
        out_specs=pl.BlockSpec(memory_space=pl.ANY),
        scratch_shapes=[
            pltpu.VMEM((n, 2, 32 * PITCH, 128), F32),
            pltpu.VMEM((n, 16, 32, 8, 128), BF16),
            pltpu.SemaphoreType.DMA((n, 4)),
        ],
        input_output_aliases={len(args) + 1: 0},
        compiler_params=pltpu.CompilerParams(vmem_limit_bytes=24 << 20),
        cost_estimate=pl.CostEstimate(flops=n << 31, bytes_accessed=n << 20, transcendentals=0),
        name="chunk",
    )(jnp.stack(places), *args, out)


def empty_kernel(out_ref):
    pass


def empty(shape):
    return pl.pallas_call(
        empty_kernel,
        out_shape=jax.ShapeDtypeStruct(shape, BF16),
        out_specs=pl.BlockSpec(memory_space=pl.ANY),
        name="empty",
    )()


def spread_table():
    table = np.zeros((2, 2, 4, 2, 4, 2, 16, 8), np.float32)
    for u in range(2):
        for g in range(2):
            for m in range(4):
                for o in range(4):
                    table[u, g, m, u, o, g, 4 * m + o, :] = 1.0
    return jnp.asarray(table.reshape(2, 64, 256), BF16)


def on_device(occupied, virtual, coulomb, transfer_pairs, shifts):
    points = 64
    z = lax.axis_index("kp")
    got = lax.all_to_all(open_up(transfer_pairs, virtual[0], occupied[0]), "ka", 0, 0, tiled=False)
    picked = pick_virtual(got)
    occ = pick_occupied(got, picked)
    vir = lax.all_to_all(picked, ("ka", "ga"), 0, 0, tiled=False)

    def shifted(block, s):
        return lax.ppermute(block, "kp", [(i, (i + s) % 8) for i in range(8)])

    near = jnp.stack([occ, shifted(occ, 1), shifted(occ, -1)])
    vir, near = lax.optimization_barrier((vir, near))
    occ = [near, shifted(near, 3), shifted(near, -3)]
    occ = lax.all_to_all(deal(z.reshape(1), occ), ("ka", "ga"), 0, 0, tiled=False)

    grid = jnp.arange(points, dtype=jnp.int32)
    cosine, sine_part = phase_angle_parts(points)
    planes = 8 * z + jnp.arange(8, dtype=jnp.int32)
    col_cos = jnp.take(cosine, planes, axis=0).astype(BF16).astype(F32).T
    col_sin = jnp.take(sine_part, planes, axis=0).astype(BF16).astype(F32).T
    turn_x = ((shifts[0, 0] * grid) % points).astype(F32) * (2.0 * math.pi / points)
    turn_y = ((shifts[0, 1] * grid) % points).astype(F32) * (2.0 * math.pi / points)
    cx, sx = jnp.cos(turn_x)[:, None], -jnp.sin(turn_x)[:, None]
    tab_cos = jnp.tile(col_cos * cx + col_sin * sx, (1, 16)).reshape(2, 32, 128)
    tab_sin = jnp.tile(col_cos * sx - col_sin * cx, (1, 16)).reshape(2, 32, 128)
    column = jnp.stack([jnp.cos(turn_y), -jnp.sin(turn_y)])
    scale = lax.dynamic_slice_in_dim(coulomb[0], 8 * z, 8, 0)
    scale = jnp.concatenate([scale, scale], 1) * (1.0 / points)
    row_table = row_table_of(points)

    forward = [(i, (i + 1) % 8) for i in range(8)]
    backward = [(i, (i - 1) % 8) for i in range(8)]
    weights = weights_of(column, occ, spread_table(), tab_cos, tab_sin)

    def add(shifted, virs, out):
        return chunk([(z - s) % 8 for s in shifted], virs, weights, row_table, scale, out)

    out = add([0], [[vir]], empty((16, 256, 8, 128)))
    ahead = behind = vir
    for s in range(1, 4):
        ahead = lax.ppermute(ahead, "kp", forward)
        behind = lax.ppermute(behind, "kp", backward)
        out = add([s, -s], [[ahead], [behind]], out)
    lower = lax.ppermute(ahead[:16], "kp", forward)
    higher = lax.ppermute(behind[16:], "kp", backward)
    out = add([4], [[lower, higher]], out)
    return out[None]


def solution(mesh):
    in_specs = (
        P("ka", "kp", "ga", None),
        P("ka", "kp", "ga", None),
        P("ka", None, None),
        P("ka", None),
        P("ka", None),
    )
    out_specs = P("ka", "ga", None, "kp", None)
    return jax.shard_map(
        on_device, mesh=mesh, in_specs=in_specs, out_specs=out_specs, check_vma=False
    )
```

```python
import functools
import math

import jax
import jax.numpy as jnp
import numpy as np
from jax import lax
from jax.experimental import pallas as pl
from jax.experimental.pallas import tpu as pltpu
from jax.sharding import PartitionSpec as P

F32 = jnp.float32
PITCH = 72
BF16 = jnp.bfloat16
VMEM = pltpu.VMEM
SMEM = pltpu.SMEM


def phase_angle_parts(points):
    index = jnp.arange(points, dtype=jnp.int32)
    windings = index[:, None] * index[None, :] % points
    angles = windings.astype(F32) * (2.0 * math.pi / points)
    return (jnp.cos(angles), jnp.sin(angles))


def row_table_of(points):
    cosine, sine_part = phase_angle_parts(points)
    upper_rows = jnp.concatenate([cosine, -sine_part], 1)
    lower_rows = jnp.concatenate([sine_part, cosine], 1)
    return jnp.concatenate([upper_rows, lower_rows], 0).astype(BF16)


def turn_orbitals(orb_ref, spread):
    norb = orb_ref.shape[0]
    pitch = spread.shape[0] // 32
    for g in range(norb // 4):
        turned = orb_ref[4 * g : 4 * g + 4].reshape(128, 128).astype(F32).T
        for o in range(4):
            lanes = [turned[32 * t : 32 * t + 32, 32 * o : 32 * o + 32] for t in range(4)]
            spread[pl.ds(4 * g + o, 32, stride=pitch), :] = jnp.concatenate(lanes, 1)
    rows = [spread[pitch * yp : pitch * yp + norb] for yp in range(32)]
    return jnp.concatenate(rows, 0).reshape(16, 2 * norb, 128)


def open_kernel(pairs_ref, vir_ref, occ_ref, out_ref, spread, spread_occ):
    out_ref[:, :64] = turn_orbitals(vir_ref, spread).astype(BF16)
    row = lax.broadcasted_iota(jnp.int32, (16, 8, 128), 1)
    told = jnp.where(row == 0, pairs_ref[0, 0], jnp.where(row == 1, pairs_ref[0, 1], 0))
    rest = [turn_orbitals(occ_ref, spread_occ), told.astype(F32)]
    out_ref[:, 64:] = jnp.concatenate(rest, 1).astype(BF16)


def open_up(pairs, virtual, occupied):
    return pl.pallas_call(
        open_kernel,
        out_shape=jax.ShapeDtypeStruct((16, 80, 128), BF16),
        in_specs=[pl.BlockSpec(memory_space=SMEM)] + [pl.BlockSpec(memory_space=VMEM)] * 2,
        out_specs=pl.BlockSpec(memory_space=VMEM),
        scratch_shapes=[pltpu.VMEM((32 * 40, 128), F32), pltpu.VMEM((32 * 8, 128), F32)],
        name="open_up",
    )(pairs, virtual, occupied)


def pick_kernel(got_ref, vir_ref, occ_ref):
    points = [got_ref[q, 64:].astype(F32).astype(jnp.int32) for q in range(16)]
    for q in range(16):
        vir_ref[q] = got_ref[points[q][9, 0], :64]
    for q in range(0, 16, 2):
        two = [got_ref[points[q + n][8, 0], 64:].astype(F32)[:8] for n in range(2)]
        occ_ref[q // 2] = jnp.concatenate(two, 0).astype(BF16)


def pick(got):
    return pl.pallas_call(
        pick_kernel,
        out_shape=[jax.ShapeDtypeStruct((16, 64, 128), BF16), jax.ShapeDtypeStruct((8, 16, 128), BF16)],
        in_specs=[pl.BlockSpec(memory_space=VMEM)],
        out_specs=[pl.BlockSpec(memory_space=VMEM)] * 2,
        name="pick",
    )(got)


CAME_BY = ((0, 4), (7, 3), (1, 5), (6, 2))


def deal_kernel(z_ref, *refs):
    got_refs, (out_ref, held) = refs[:4], refs[4:]
    for got_ref, steps in zip(got_refs, CAME_BY):
        for n in range(2):
            held[steps[n]] = got_ref[n].astype(F32)
    for g in range(2):
        for m in range(0, 4, 2):
            sources = [(4 * g + m + n - z_ref[0] + 8) % 8 for n in range(2)]
            for q in range(16):
                spot = 8 * (q % 2)
                rows = jnp.concatenate([held[s, q // 2, spot : spot + 8] for s in sources], 0)
                out_ref[2 * q + g, 8 * m : 8 * m + 16] = rows.astype(BF16)


def deal(z, got):
    return pl.pallas_call(
        deal_kernel,
        out_shape=jax.ShapeDtypeStruct((32, 32, 128), BF16),
        in_specs=[pl.BlockSpec(memory_space=SMEM)] + [pl.BlockSpec(memory_space=VMEM)] * 4,
        out_specs=pl.BlockSpec(memory_space=VMEM),
        scratch_shapes=[pltpu.VMEM((8, 8, 16, 128), F32)],
        name="deal",
    )(z, *got)


def weight_kernel(half_ref, column_ref, occ_ref, spread_ref, cos_ref, sin_ref, out_ref):
    half = half_ref[0]

    def step(yp, carry):
        piece, odd = yp // 2, yp % 2
        occ = jnp.concatenate([occ_ref[2 * piece + half], occ_ref[2 * piece + 1 - half]], 0)
        wide = lax.dot_general(occ, spread_ref[odd], (((0,), (0,)), ((), ())), preferred_element_type=F32)
        for g in range(2):
            ac, as_ = cos_ref[g], sin_ref[g]
            for u in range(2):
                c, s = column_ref[0, 32 * u + yp], column_ref[1, 32 * u + yp]
                tr = ac * c - as_ * s
                ti = as_ * c + ac * s
                real = wide[32 * u : 32 * u + 32, 128 * g : 128 * g + 128]
                imag = wide[64 + 32 * u : 96 + 32 * u, 128 * g : 128 * g + 128]
                wr = (real * tr + imag * ti).astype(BF16)
                wi = real * ti - imag * tr
                base = 128 * g + 32 * u
                out_ref[yp, base : base + 32, :128] = wr
                out_ref[yp, base : base + 32, 128:] = wi.astype(BF16)
                out_ref[yp, base + 64 : base + 96, :128] = (-wi).astype(BF16)
                out_ref[yp, base + 64 : base + 96, 128:] = wr
        return carry

    lax.fori_loop(0, 32, step, 0, unroll=8)


def weights_of(half, column, occ, spread, cosine, sine_part):
    return pl.pallas_call(
        weight_kernel,
        out_shape=jax.ShapeDtypeStruct((32, 256, 256), BF16),
        in_specs=[pl.BlockSpec(memory_space=SMEM)] * 2 + [pl.BlockSpec(memory_space=VMEM)] * 4,
        out_specs=pl.BlockSpec(memory_space=VMEM),
        compiler_params=pltpu.CompilerParams(vmem_limit_bytes=24 << 20),
        cost_estimate=pl.CostEstimate(flops=32 * 2 * 128 * 32 * 256, bytes_accessed=6 << 20, transcendentals=0),
        name="weights",
    )(half, column, occ, spread, cosine, sine_part)


def chunk_kernel(parts, place_ref, *refs):
    vir_refs, (weight_ref, row_ref, scale_ref, _, out_ref, total, ready, sems) = refs[:-8], refs[-8:]
    lane = lax.broadcasted_iota(jnp.int32, (32, 256), 1)
    upper = (lane // 32) % 2 == 0
    copies = []
    for n, part in enumerate(parts):
        here = vir_refs[: 2 * part]
        vir_refs = vir_refs[2 * part :]
        yp = 0
        for own_ref, other_ref in zip(here[0::2], here[1::2]):
            for step in range(own_ref.shape[0]):
                both = jnp.concatenate([own_ref[step], other_ref[step]], 1)
                nought = jnp.zeros_like(both)
                split = jnp.concatenate([jnp.where(upper, both, nought), jnp.where(upper, nought, both)], 0)
                sums = jnp.dot(split, weight_ref[yp], preferred_element_type=F32)
                for u in range(2):
                    for c in range(2):
                        block = sums[32 * u : 32 * u + 32, 128 * c : 128 * c + 128]
                        total[n, c, pl.ds(32 * u + yp, 32, stride=PITCH), :] = block
                yp += 1

        for a in range(32):
            left = jnp.concatenate([total[n, c, PITCH * a : PITCH * a + 64, :] for c in range(2)], 0).astype(BF16)
            result = lax.dot_general(left, row_ref[...], (((0,), (0,)), ((), ())), preferred_element_type=F32)
            ready[n, :, a] = (result.reshape(16, 8, 128) * scale_ref[...][None]).astype(BF16)
            if a % 8 == 7:
                copy = pltpu.make_async_copy(
                    ready.at[n, :, pl.ds(a - 7, 8)],
                    out_ref.at[:, pl.ds(32 * place_ref[n] + (a - 7), 8)],
                    sems.at[n, a // 8],
                )
                copy.start()
                copies.append(copy)
    for copy in copies:
        copy.wait()


def chunk(places, virs, weights, row_table, scale, out):
    n = len(virs)
    args = [v for vir in virs for v in vir] + [weights, row_table, scale]
    return pl.pallas_call(
        functools.partial(chunk_kernel, [len(vir) // 2 for vir in virs]),
        out_shape=jax.ShapeDtypeStruct(out.shape, BF16),
        in_specs=[pl.BlockSpec(memory_space=SMEM)]
        + [pl.BlockSpec(memory_space=VMEM)] * len(args)
        + [pl.BlockSpec(memory_space=pl.ANY)],
        out_specs=pl.BlockSpec(memory_space=pl.ANY),
        scratch_shapes=[
            pltpu.VMEM((n, 2, 32 * PITCH, 128), F32),
            pltpu.VMEM((n, 16, 32, 8, 128), BF16),
            pltpu.SemaphoreType.DMA((n, 4)),
        ],
        input_output_aliases={len(args) + 1: 0},
        compiler_params=pltpu.CompilerParams(vmem_limit_bytes=24 << 20),
        cost_estimate=pl.CostEstimate(flops=n << 31, bytes_accessed=n << 20, transcendentals=0),
        name="chunk",
    )(jnp.stack(places), *args, out)


def empty_kernel(out_ref):
    pass


def empty(shape):
    return pl.pallas_call(
        empty_kernel,
        out_shape=jax.ShapeDtypeStruct(shape, BF16),
        out_specs=pl.BlockSpec(memory_space=pl.ANY),
        name="empty",
    )()


def spread_table():
    table = np.zeros((2, 2, 4, 2, 4, 2, 16, 8), np.float32)
    for u in range(2):
        for g in range(2):
            for m in range(4):
                for o in range(4):
                    table[u, g, m, u, o, g, 4 * m + o, :] = 1.0
    return jnp.asarray(table.reshape(2, 64, 256), BF16)


def on_device(occupied, virtual, coulomb, transfer_pairs, shifts):
    points = 64
    z, half = lax.axis_index("kp"), lax.axis_index("ga")
    got = lax.all_to_all(open_up(transfer_pairs, virtual[0], occupied[0]), "ka", 0, 0, tiled=False)
    picked, occ = pick(got)
    own = lax.all_to_all(picked, "ka", 0, 0, tiled=False).reshape(32, 32, 128)
    two = jnp.stack([occ, lax.ppermute(occ, "kp", [(i, (i + 4) % 8) for i in range(8)])])
    occ = [two] + [lax.ppermute(two, "kp", [(i, (i + s) % 8) for i in range(8)]) for s in (1, -1, 2)]
    occ = lax.all_to_all(deal(z.reshape(1), occ), ("ka", "ga"), 0, 0, tiled=False)

    grid = jnp.arange(points, dtype=jnp.int32)
    cosine, sine_part = phase_angle_parts(points)
    planes = 8 * z + jnp.arange(8, dtype=jnp.int32)
    col_cos = jnp.take(cosine, planes, axis=0).astype(BF16).astype(F32).T
    col_sin = jnp.take(sine_part, planes, axis=0).astype(BF16).astype(F32).T
    turn_x = ((shifts[0, 0] * grid) % points).astype(F32) * (2.0 * math.pi / points)
    turn_y = ((shifts[0, 1] * grid) % points).astype(F32) * (2.0 * math.pi / points)
    cx, sx = jnp.cos(turn_x)[:, None], -jnp.sin(turn_x)[:, None]
    tab_cos = jnp.tile(col_cos * cx + col_sin * sx, (1, 16)).reshape(2, 32, 128)
    tab_sin = jnp.tile(col_cos * sx - col_sin * cx, (1, 16)).reshape(2, 32, 128)
    column = jnp.stack([jnp.cos(turn_y), -jnp.sin(turn_y)])
    scale = lax.dynamic_slice_in_dim(coulomb[0], 8 * z, 8, 0)
    scale = jnp.concatenate([scale, scale], 1) * (1.0 / points)
    row_table = row_table_of(points)

    forward = [(i, (i + 1) % 8) for i in range(8)]
    backward = [(i, (i - 1) % 8) for i in range(8)]
    tab_cos = jnp.where(half == 0, tab_cos, tab_cos[::-1])
    tab_sin = jnp.where(half == 0, tab_sin, tab_sin[::-1])
    weights = weights_of(half.reshape(1), column, occ, spread_table(), tab_cos, tab_sin)

    def add(shifted, virs, out):
        return chunk([(z - s) % 8 for s in shifted], virs, weights, row_table, scale, out)

    other = lax.ppermute(own, "ga", [(0, 1), (1, 0)])
    out = add([0], [[own, other]], empty((16, 256, 8, 128)))
    ahead = behind = [own, other]
    for s in range(1, 4):
        ahead = [lax.ppermute(v, "kp", forward) for v in ahead]
        behind = [lax.ppermute(v, "kp", backward) for v in behind]
        out = add([s, -s], [ahead, behind], out)
    lower = [lax.ppermute(v[:16], "kp", forward) for v in ahead]
    higher = [lax.ppermute(v[16:], "kp", backward) for v in behind]
    out = add([4], [lower + higher], out)
    return out[None]


def solution(mesh):
    in_specs = (
        P("ka", "kp", "ga", None),
        P("ka", "kp", "ga", None),
        P("ka", None, None),
        P("ka", None),
        P("ka", None),
    )
    out_specs = P("ka", "ga", None, "kp", None)
    return jax.shard_map(
        on_device, mesh=mesh, in_specs=in_specs, out_specs=out_specs, check_vma=False
    )
```

```python
import functools
import math

import jax
import jax.numpy as jnp
import numpy as np
from jax import lax
from jax.experimental import pallas as pl
from jax.experimental.pallas import tpu as pltpu
from jax.sharding import PartitionSpec as P

F32 = jnp.float32
PITCH = 72
BF16 = jnp.bfloat16
VMEM = pltpu.VMEM
SMEM = pltpu.SMEM


def phase_angle_parts(points):
    index = jnp.arange(points, dtype=jnp.int32)
    windings = index[:, None] * index[None, :] % points
    angles = windings.astype(F32) * (2.0 * math.pi / points)
    return (jnp.cos(angles), jnp.sin(angles))


def row_table_of(points):
    cosine, sine_part = phase_angle_parts(points)
    upper_rows = jnp.concatenate([cosine, -sine_part], 1)
    lower_rows = jnp.concatenate([sine_part, cosine], 1)
    return jnp.concatenate([upper_rows, lower_rows], 0).astype(BF16)


def turn_orbitals(orb_ref, spread):
    norb = orb_ref.shape[0]
    pitch = spread.shape[0] // 32
    for g in range(norb // 4):
        turned = orb_ref[4 * g : 4 * g + 4].reshape(128, 128).astype(F32).T
        for o in range(4):
            lanes = [turned[32 * t : 32 * t + 32, 32 * o : 32 * o + 32] for t in range(4)]
            spread[pl.ds(4 * g + o, 32, stride=pitch), :] = jnp.concatenate(lanes, 1)
    rows = [spread[pitch * yp : pitch * yp + norb] for yp in range(32)]
    return jnp.concatenate(rows, 0).reshape(16, 2 * norb, 128)


def open_kernel(pairs_ref, vir_ref, occ_ref, out_ref, spread, spread_occ):
    out_ref[:, :64] = turn_orbitals(vir_ref, spread).astype(BF16)
    row = lax.broadcasted_iota(jnp.int32, (16, 8, 128), 1)
    told = jnp.where(row == 0, pairs_ref[0, 0], jnp.where(row == 1, pairs_ref[0, 1], 0))
    rest = [turn_orbitals(occ_ref, spread_occ), told.astype(F32)]
    out_ref[:, 64:] = jnp.concatenate(rest, 1).astype(BF16)


def open_up(pairs, virtual, occupied):
    return pl.pallas_call(
        open_kernel,
        out_shape=jax.ShapeDtypeStruct((16, 80, 128), BF16),
        in_specs=[pl.BlockSpec(memory_space=SMEM)] + [pl.BlockSpec(memory_space=VMEM)] * 2,
        out_specs=pl.BlockSpec(memory_space=VMEM),
        scratch_shapes=[pltpu.VMEM((32 * 40, 128), F32), pltpu.VMEM((32 * 8, 128), F32)],
        name="open_up",
    )(pairs, virtual, occupied)


def pick_kernel(got_ref, vir_ref, occ_ref):
    points = [got_ref[q, 64:].astype(F32).astype(jnp.int32) for q in range(16)]
    for q in range(16):
        for g in range(2):
            vir_ref[2 * q + g] = got_ref[points[q][9, 0], :64]
    for q in range(0, 16, 2):
        two = [got_ref[points[q + n][8, 0], 64:].astype(F32)[:8] for n in range(2)]
        occ_ref[q // 2] = jnp.concatenate(two, 0).astype(BF16)


def pick(got):
    return pl.pallas_call(
        pick_kernel,
        out_shape=[jax.ShapeDtypeStruct((32, 64, 128), BF16), jax.ShapeDtypeStruct((8, 16, 128), BF16)],
        in_specs=[pl.BlockSpec(memory_space=VMEM)],
        out_specs=[pl.BlockSpec(memory_space=VMEM)] * 2,
        name="pick",
    )(got)


CAME_BY = ((0, 4), (7, 3), (1, 5), (6, 2))


def deal_kernel(z_ref, *refs):
    got_refs, (out_ref, held) = refs[:4], refs[4:]
    for got_ref, steps in zip(got_refs, CAME_BY):
        for n in range(2):
            held[steps[n]] = got_ref[n].astype(F32)
    for g in range(2):
        for m in range(0, 4, 2):
            sources = [(4 * g + m + n - z_ref[0] + 8) % 8 for n in range(2)]
            for q in range(16):
                spot = 8 * (q % 2)
                rows = jnp.concatenate([held[s, q // 2, spot : spot + 8] for s in sources], 0)
                out_ref[2 * q + g, 8 * m : 8 * m + 16] = rows.astype(BF16)


def deal(z, got):
    return pl.pallas_call(
        deal_kernel,
        out_shape=jax.ShapeDtypeStruct((32, 32, 128), BF16),
        in_specs=[pl.BlockSpec(memory_space=SMEM)] + [pl.BlockSpec(memory_space=VMEM)] * 4,
        out_specs=pl.BlockSpec(memory_space=VMEM),
        scratch_shapes=[pltpu.VMEM((8, 8, 16, 128), F32)],
        name="deal",
    )(z, *got)


def weight_kernel(column_ref, occ_ref, spread_ref, cos_ref, sin_ref, out_ref):
    def step(yp, carry):
        piece, odd = yp // 2, yp % 2
        occ = jnp.concatenate([occ_ref[2 * piece], occ_ref[2 * piece + 1]], 0)
        wide = lax.dot_general(occ, spread_ref[odd], (((0,), (0,)), ((), ())), preferred_element_type=F32)
        for g in range(2):
            ac, as_ = cos_ref[g], sin_ref[g]
            for u in range(2):
                c, s = column_ref[0, 32 * u + yp], column_ref[1, 32 * u + yp]
                tr = ac * c - as_ * s
                ti = as_ * c + ac * s
                real = wide[32 * u : 32 * u + 32, 128 * g : 128 * g + 128]
                imag = wide[64 + 32 * u : 96 + 32 * u, 128 * g : 128 * g + 128]
                wr = (real * tr + imag * ti).astype(BF16)
                wi = real * ti - imag * tr
                base = 128 * g + 32 * u
                out_ref[yp, base : base + 32, :128] = wr
                out_ref[yp, base : base + 32, 128:] = wi.astype(BF16)
                out_ref[yp, base + 64 : base + 96, :128] = (-wi).astype(BF16)
                out_ref[yp, base + 64 : base + 96, 128:] = wr
        return carry

    lax.fori_loop(0, 32, step, 0, unroll=8)


def weights_of(column, occ, spread, cosine, sine_part):
    return pl.pallas_call(
        weight_kernel,
        out_shape=jax.ShapeDtypeStruct((32, 256, 256), BF16),
        in_specs=[pl.BlockSpec(memory_space=SMEM)] + [pl.BlockSpec(memory_space=VMEM)] * 4,
        out_specs=pl.BlockSpec(memory_space=VMEM),
        compiler_params=pltpu.CompilerParams(vmem_limit_bytes=24 << 20),
        cost_estimate=pl.CostEstimate(flops=32 * 2 * 128 * 32 * 256, bytes_accessed=6 << 20, transcendentals=0),
        name="weights",
    )(column, occ, spread, cosine, sine_part)


def chunk_kernel(parts, place_ref, *refs):
    vir_refs, (weight_ref, row_ref, scale_ref, _, out_ref, total, ready, sems) = refs[:-8], refs[-8:]
    lane = lax.broadcasted_iota(jnp.int32, (32, 256), 1)
    upper = (lane // 32) % 2 == 0
    copies = []
    for n, part in enumerate(parts):
        here = vir_refs[:part]
        vir_refs = vir_refs[part:]
        yp = 0
        for vir_ref in here:
            for step in range(vir_ref.shape[0]):
                rows = slice(32 * (step % 2), 32 * (step % 2) + 32)
                both = [vir_ref[step // 2 * 2 + g, rows] for g in range(2)]
                both = jnp.concatenate(both, 1)
                nought = jnp.zeros_like(both)
                split = jnp.concatenate([jnp.where(upper, both, nought), jnp.where(upper, nought, both)], 0)
                sums = jnp.dot(split, weight_ref[yp], preferred_element_type=F32)
                for u in range(2):
                    for c in range(2):
                        block = sums[32 * u : 32 * u + 32, 128 * c : 128 * c + 128]
                        total[n, c, pl.ds(32 * u + yp, 32, stride=PITCH), :] = block
                yp += 1

        for a in range(32):
            left = jnp.concatenate([total[n, c, PITCH * a : PITCH * a + 64, :] for c in range(2)], 0).astype(BF16)
            result = lax.dot_general(left, row_ref[...], (((0,), (0,)), ((), ())), preferred_element_type=F32)
            ready[n, :, a] = (result.reshape(16, 8, 128) * scale_ref[...][None]).astype(BF16)
            if a % 8 == 7:
                copy = pltpu.make_async_copy(
                    ready.at[n, :, pl.ds(a - 7, 8)],
                    out_ref.at[:, pl.ds(32 * place_ref[n] + (a - 7), 8)],
                    sems.at[n, a // 8],
                )
                copy.start()
                copies.append(copy)
    for copy in copies:
        copy.wait()


def chunk(places, virs, weights, row_table, scale, out):
    n = len(virs)
    args = [v for vir in virs for v in vir] + [weights, row_table, scale]
    return pl.pallas_call(
        functools.partial(chunk_kernel, [len(vir) for vir in virs]),
        out_shape=jax.ShapeDtypeStruct(out.shape, BF16),
        in_specs=[pl.BlockSpec(memory_space=SMEM)]
        + [pl.BlockSpec(memory_space=VMEM)] * len(args)
        + [pl.BlockSpec(memory_space=pl.ANY)],
        out_specs=pl.BlockSpec(memory_space=pl.ANY),
        scratch_shapes=[
            pltpu.VMEM((n, 2, 32 * PITCH, 128), F32),
            pltpu.VMEM((n, 16, 32, 8, 128), BF16),
            pltpu.SemaphoreType.DMA((n, 4)),
        ],
        input_output_aliases={len(args) + 1: 0},
        compiler_params=pltpu.CompilerParams(vmem_limit_bytes=24 << 20),
        cost_estimate=pl.CostEstimate(flops=n << 31, bytes_accessed=n << 20, transcendentals=0),
        name="chunk",
    )(jnp.stack(places), *args, out)


def empty_kernel(out_ref):
    pass


def empty(shape):
    return pl.pallas_call(
        empty_kernel,
        out_shape=jax.ShapeDtypeStruct(shape, BF16),
        out_specs=pl.BlockSpec(memory_space=pl.ANY),
        name="empty",
    )()


def spread_table():
    table = np.zeros((2, 2, 4, 2, 4, 2, 16, 8), np.float32)
    for u in range(2):
        for g in range(2):
            for m in range(4):
                for o in range(4):
                    table[u, g, m, u, o, g, 4 * m + o, :] = 1.0
    return jnp.asarray(table.reshape(2, 64, 256), BF16)


def on_device(occupied, virtual, coulomb, transfer_pairs, shifts):
    points = 64
    z = lax.axis_index("kp")
    got = lax.all_to_all(open_up(transfer_pairs, virtual[0], occupied[0]), "ka", 0, 0, tiled=False)
    picked, occ = pick(got)
    vir = lax.all_to_all(picked, ("ka", "ga"), 0, 0, tiled=False)
    two = jnp.stack([occ, lax.ppermute(occ, "kp", [(i, (i + 4) % 8) for i in range(8)])])
    occ = [two] + [lax.ppermute(two, "kp", [(i, (i + s) % 8) for i in range(8)]) for s in (1, -1, 2)]
    occ = lax.all_to_all(deal(z.reshape(1), occ), ("ka", "ga"), 0, 0, tiled=False)

    grid = jnp.arange(points, dtype=jnp.int32)
    cosine, sine_part = phase_angle_parts(points)
    planes = 8 * z + jnp.arange(8, dtype=jnp.int32)
    col_cos = jnp.take(cosine, planes, axis=0).astype(BF16).astype(F32).T
    col_sin = jnp.take(sine_part, planes, axis=0).astype(BF16).astype(F32).T
    turn_x = ((shifts[0, 0] * grid) % points).astype(F32) * (2.0 * math.pi / points)
    turn_y = ((shifts[0, 1] * grid) % points).astype(F32) * (2.0 * math.pi / points)
    cx, sx = jnp.cos(turn_x)[:, None], -jnp.sin(turn_x)[:, None]
    tab_cos = jnp.tile(col_cos * cx + col_sin * sx, (1, 16)).reshape(2, 32, 128)
    tab_sin = jnp.tile(col_cos * sx - col_sin * cx, (1, 16)).reshape(2, 32, 128)
    column = jnp.stack([jnp.cos(turn_y), -jnp.sin(turn_y)])
    scale = lax.dynamic_slice_in_dim(coulomb[0], 8 * z, 8, 0)
    scale = jnp.concatenate([scale, scale], 1) * (1.0 / points)
    row_table = row_table_of(points)

    forward = [(i, (i + 1) % 8) for i in range(8)]
    backward = [(i, (i - 1) % 8) for i in range(8)]
    weights = weights_of(column, occ, spread_table(), tab_cos, tab_sin)

    def add(shifted, virs, out):
        return chunk([(z - s) % 8 for s in shifted], virs, weights, row_table, scale, out)

    ahead = behind = [vir[:16], vir[16:]]
    out = add([0], [ahead], empty((16, 256, 8, 128)))
    for s in range(1, 4):
        ahead = [lax.ppermute(v, "kp", forward) for v in ahead]
        behind = [lax.ppermute(v, "kp", backward) for v in behind]
        out = add([s, -s], [ahead, behind], out)
    last = []
    for a, b in zip(ahead, behind):
        last += [lax.ppermute(a[:8], "kp", forward), lax.ppermute(b[8:], "kp", backward)]
    out = add([4], [last], out)
    return out[None]


def solution(mesh):
    in_specs = (
        P("ka", "kp", "ga", None),
        P("ka", "kp", "ga", None),
        P("ka", None, None),
        P("ka", None),
        P("ka", None),
    )
    out_specs = P("ka", "ga", None, "kp", None)
    return jax.shard_map(
        on_device, mesh=mesh, in_specs=in_specs, out_specs=out_specs, check_vma=False
    )
```

```python
import functools
import math

import jax
import jax.numpy as jnp
import numpy as np
from jax import lax
from jax.experimental import pallas as pl
from jax.experimental.pallas import tpu as pltpu
from jax.sharding import PartitionSpec as P

F32 = jnp.float32
PITCH = 72
BF16 = jnp.bfloat16
VMEM = pltpu.VMEM
SMEM = pltpu.SMEM


def phase_angle_parts(points):
    index = jnp.arange(points, dtype=jnp.int32)
    windings = index[:, None] * index[None, :] % points
    angles = windings.astype(F32) * (2.0 * math.pi / points)
    return (jnp.cos(angles), jnp.sin(angles))


def row_table_of(points):
    cosine, sine_part = phase_angle_parts(points)
    upper_rows = jnp.concatenate([cosine, -sine_part], 1)
    lower_rows = jnp.concatenate([sine_part, cosine], 1)
    return jnp.concatenate([upper_rows, lower_rows], 0).astype(BF16)


def turn_orbitals(orb_ref, spread):
    norb = orb_ref.shape[0]
    pitch = spread.shape[0] // 32
    for g in range(norb // 4):
        turned = orb_ref[4 * g : 4 * g + 4].reshape(128, 128).astype(F32).T
        for o in range(4):
            lanes = [turned[32 * t : 32 * t + 32, 32 * o : 32 * o + 32] for t in range(4)]
            spread[pl.ds(4 * g + o, 32, stride=pitch), :] = jnp.concatenate(lanes, 1)
    rows = [spread[pitch * yp : pitch * yp + norb] for yp in range(32)]
    return jnp.concatenate(rows, 0).reshape(16, 2 * norb, 128)


def open_kernel(pairs_ref, vir_ref, occ_ref, out_ref, spread, spread_occ):
    out_ref[:, :64] = turn_orbitals(vir_ref, spread).astype(BF16)
    row = lax.broadcasted_iota(jnp.int32, (16, 8, 128), 1)
    told = jnp.where(row == 0, pairs_ref[0, 0], jnp.where(row == 1, pairs_ref[0, 1], 0))
    rest = [turn_orbitals(occ_ref, spread_occ), told.astype(F32)]
    out_ref[:, 64:] = jnp.concatenate(rest, 1).astype(BF16)


def open_up(pairs, virtual, occupied):
    return pl.pallas_call(
        open_kernel,
        out_shape=jax.ShapeDtypeStruct((16, 80, 128), BF16),
        in_specs=[pl.BlockSpec(memory_space=SMEM)] + [pl.BlockSpec(memory_space=VMEM)] * 2,
        out_specs=pl.BlockSpec(memory_space=VMEM),
        scratch_shapes=[pltpu.VMEM((32 * 40, 128), F32), pltpu.VMEM((32 * 8, 128), F32)],
        name="open_up",
    )(pairs, virtual, occupied)


def pick_kernel(got_ref, vir_ref, occ_ref):
    points = [got_ref[q, 64:].astype(F32).astype(jnp.int32) for q in range(16)]
    for q in range(16):
        for g in range(2):
            vir_ref[2 * q + g] = got_ref[points[q][9, 0], :64]
    for q in range(0, 16, 2):
        two = [got_ref[points[q + n][8, 0], 64:].astype(F32)[:8] for n in range(2)]
        occ_ref[q // 2] = jnp.concatenate(two, 0).astype(BF16)


def pick(got):
    return pl.pallas_call(
        pick_kernel,
        out_shape=[jax.ShapeDtypeStruct((32, 64, 128), BF16), jax.ShapeDtypeStruct((8, 16, 128), BF16)],
        in_specs=[pl.BlockSpec(memory_space=VMEM)],
        out_specs=[pl.BlockSpec(memory_space=VMEM)] * 2,
        name="pick",
    )(got)


CAME_BY = ((0, 4), (7, 3), (1, 5), (6, 2))


def deal_kernel(z_ref, *refs):
    got_refs, (out_ref, held) = refs[:4], refs[4:]
    for got_ref, steps in zip(got_refs, CAME_BY):
        for n in range(2):
            held[steps[n]] = got_ref[n].astype(F32)
    for g in range(2):
        for m in range(0, 4, 2):
            sources = [(4 * g + m + n - z_ref[0] + 8) % 8 for n in range(2)]
            for q in range(16):
                spot = 8 * (q % 2)
                rows = jnp.concatenate([held[s, q // 2, spot : spot + 8] for s in sources], 0)
                out_ref[2 * q + g, 8 * m : 8 * m + 16] = rows.astype(BF16)


def deal(z, got):
    return pl.pallas_call(
        deal_kernel,
        out_shape=jax.ShapeDtypeStruct((32, 32, 128), BF16),
        in_specs=[pl.BlockSpec(memory_space=SMEM)] + [pl.BlockSpec(memory_space=VMEM)] * 4,
        out_specs=pl.BlockSpec(memory_space=VMEM),
        scratch_shapes=[pltpu.VMEM((8, 8, 16, 128), F32)],
        name="deal",
    )(z, *got)


def weight_kernel(column_ref, occ_ref, spread_ref, cos_ref, sin_ref, out_ref):
    def step(yp, carry):
        piece, odd = yp // 2, yp % 2
        occ = jnp.concatenate([occ_ref[2 * piece], occ_ref[2 * piece + 1]], 0)
        wide = lax.dot_general(occ, spread_ref[odd], (((0,), (0,)), ((), ())), preferred_element_type=F32)
        for g in range(2):
            ac, as_ = cos_ref[g], sin_ref[g]
            for u in range(2):
                c, s = column_ref[0, 32 * u + yp], column_ref[1, 32 * u + yp]
                tr = ac * c - as_ * s
                ti = as_ * c + ac * s
                real = wide[32 * u : 32 * u + 32, 128 * g : 128 * g + 128]
                imag = wide[64 + 32 * u : 96 + 32 * u, 128 * g : 128 * g + 128]
                wr = (real * tr + imag * ti).astype(BF16)
                wi = real * ti - imag * tr
                base = 128 * g + 32 * u
                out_ref[yp, base : base + 32, :128] = wr
                out_ref[yp, base : base + 32, 128:] = wi.astype(BF16)
                out_ref[yp, base + 64 : base + 96, :128] = (-wi).astype(BF16)
                out_ref[yp, base + 64 : base + 96, 128:] = wr
        return carry

    lax.fori_loop(0, 32, step, 0, unroll=8)


def weights_of(column, occ, spread, cosine, sine_part):
    return pl.pallas_call(
        weight_kernel,
        out_shape=jax.ShapeDtypeStruct((32, 256, 256), BF16),
        in_specs=[pl.BlockSpec(memory_space=SMEM)] + [pl.BlockSpec(memory_space=VMEM)] * 4,
        out_specs=pl.BlockSpec(memory_space=VMEM),
        compiler_params=pltpu.CompilerParams(vmem_limit_bytes=24 << 20),
        cost_estimate=pl.CostEstimate(flops=32 * 2 * 128 * 32 * 256, bytes_accessed=6 << 20, transcendentals=0),
        name="weights",
    )(column, occ, spread, cosine, sine_part)


def chunk_kernel(parts, place_ref, *refs):
    vir_refs, (weight_ref, row_ref, scale_ref, _, out_ref, total, ready, sems) = refs[:-8], refs[-8:]
    lane = lax.broadcasted_iota(jnp.int32, (32, 256), 1)
    upper = (lane // 32) % 2 == 0
    copies = []
    for n, part in enumerate(parts):
        here = vir_refs[:part]
        vir_refs = vir_refs[part:]
        yp = 0
        for vir_ref in here:
            for step in range(vir_ref.shape[0]):
                rows = slice(32 * (step % 2), 32 * (step % 2) + 32)
                both = [vir_ref[step // 2 * 2 + g, rows] for g in range(2)]
                both = jnp.concatenate(both, 1)
                nought = jnp.zeros_like(both)
                split = jnp.concatenate([jnp.where(upper, both, nought), jnp.where(upper, nought, both)], 0)
                sums = jnp.dot(split, weight_ref[yp], preferred_element_type=F32)
                for u in range(2):
                    for c in range(2):
                        block = sums[32 * u : 32 * u + 32, 128 * c : 128 * c + 128]
                        total[n, c, pl.ds(32 * u + yp, 32, stride=PITCH), :] = block
                yp += 1

        for a in range(32):
            left = jnp.concatenate([total[n, c, PITCH * a : PITCH * a + 64, :] for c in range(2)], 0).astype(BF16)
            result = lax.dot_general(left, row_ref[...], (((0,), (0,)), ((), ())), preferred_element_type=F32)
            ready[n, :, a] = (result.reshape(16, 8, 128) * scale_ref[...][None]).astype(BF16)
            if a % 8 == 7:
                copy = pltpu.make_async_copy(
                    ready.at[n, :, pl.ds(a - 7, 8)],
                    out_ref.at[:, pl.ds(32 * place_ref[n] + (a - 7), 8)],
                    sems.at[n, a // 8],
                )
                copy.start()
                copies.append(copy)
    for copy in copies:
        copy.wait()


def chunk(places, virs, weights, row_table, scale, out):
    n = len(virs)
    args = [v for vir in virs for v in vir] + [weights, row_table, scale]
    return pl.pallas_call(
        functools.partial(chunk_kernel, [len(vir) for vir in virs]),
        out_shape=jax.ShapeDtypeStruct(out.shape, BF16),
        in_specs=[pl.BlockSpec(memory_space=SMEM)]
        + [pl.BlockSpec(memory_space=VMEM)] * len(args)
        + [pl.BlockSpec(memory_space=pl.ANY)],
        out_specs=pl.BlockSpec(memory_space=pl.ANY),
        scratch_shapes=[
            pltpu.VMEM((n, 2, 32 * PITCH, 128), F32),
            pltpu.VMEM((n, 16, 32, 8, 128), BF16),
            pltpu.SemaphoreType.DMA((n, 4)),
        ],
        input_output_aliases={len(args) + 1: 0},
        compiler_params=pltpu.CompilerParams(vmem_limit_bytes=24 << 20),
        cost_estimate=pl.CostEstimate(flops=n << 31, bytes_accessed=n << 20, transcendentals=0),
        name="chunk",
    )(jnp.stack(places), *args, out)


def empty_kernel(out_ref):
    pass


def empty(shape):
    return pl.pallas_call(
        empty_kernel,
        out_shape=jax.ShapeDtypeStruct(shape, BF16),
        out_specs=pl.BlockSpec(memory_space=pl.ANY),
        name="empty",
    )()


def spread_table():
    table = np.zeros((2, 2, 4, 2, 4, 2, 16, 8), np.float32)
    for u in range(2):
        for g in range(2):
            for m in range(4):
                for o in range(4):
                    table[u, g, m, u, o, g, 4 * m + o, :] = 1.0
    return jnp.asarray(table.reshape(2, 64, 256), BF16)


def on_device(occupied, virtual, coulomb, transfer_pairs, shifts):
    points = 64
    z = lax.axis_index("kp")
    got = lax.all_to_all(open_up(transfer_pairs, virtual[0], occupied[0]), "ka", 0, 0, tiled=False)
    picked, occ = pick(got)
    vir = lax.all_to_all(picked, ("ka", "ga"), 0, 0, tiled=False)
    two = jnp.stack([occ, lax.ppermute(occ, "kp", [(i, (i + 4) % 8) for i in range(8)])])
    occ = [two] + [lax.ppermute(two, "kp", [(i, (i + s) % 8) for i in range(8)]) for s in (1, -1, 2)]

    grid = jnp.arange(points, dtype=jnp.int32)
    cosine, sine_part = phase_angle_parts(points)
    planes = 8 * z + jnp.arange(8, dtype=jnp.int32)
    col_cos = jnp.take(cosine, planes, axis=0).astype(BF16).astype(F32).T
    col_sin = jnp.take(sine_part, planes, axis=0).astype(BF16).astype(F32).T
    turn_x = ((shifts[0, 0] * grid) % points).astype(F32) * (2.0 * math.pi / points)
    turn_y = ((shifts[0, 1] * grid) % points).astype(F32) * (2.0 * math.pi / points)
    cx, sx = jnp.cos(turn_x)[:, None], -jnp.sin(turn_x)[:, None]
    tab_cos = jnp.tile(col_cos * cx + col_sin * sx, (1, 16)).reshape(2, 32, 128)
    tab_sin = jnp.tile(col_cos * sx - col_sin * cx, (1, 16)).reshape(2, 32, 128)
    column = jnp.stack([jnp.cos(turn_y), -jnp.sin(turn_y)])
    scale = lax.dynamic_slice_in_dim(coulomb[0], 8 * z, 8, 0)
    scale = jnp.concatenate([scale, scale], 1) * (1.0 / points)
    row_table = row_table_of(points)

    forward = [(i, (i + 1) % 8) for i in range(8)]
    backward = [(i, (i - 1) % 8) for i in range(8)]

    rounds = [([vir[:16], vir[16:]],) * 2]
    for s in range(3):
        ahead = [lax.ppermute(v, "kp", forward) for v in rounds[s][0]]
        behind = [lax.ppermute(v, "kp", backward) for v in rounds[s][1]]
        rounds.append((ahead, behind))
    occ = lax.optimization_barrier((rounds[1][0][0], *occ))[1:]
    occ = lax.all_to_all(deal(z.reshape(1), occ), ("ka", "ga"), 0, 0, tiled=False)
    weights = weights_of(column, occ, spread_table(), tab_cos, tab_sin)
    out = empty((16, 256, 8, 128))

    def add(shifted, virs, out):
        return chunk([(z - s) % 8 for s in shifted], virs, weights, row_table, scale, out)

    out = add([0], [rounds[0][0]], out)
    for s in range(1, 4):
        out = add([s, -s], rounds[s], out)
    last = []
    for a, b in zip(ahead, behind):
        last += [lax.ppermute(a[:8], "kp", forward), lax.ppermute(b[8:], "kp", backward)]
    out = add([4], [last], out)
    return out[None]


def solution(mesh):
    in_specs = (
        P("ka", "kp", "ga", None),
        P("ka", "kp", "ga", None),
        P("ka", None, None),
        P("ka", None),
        P("ka", None),
    )
    out_specs = P("ka", "ga", None, "kp", None)
    return jax.shard_map(
        on_device, mesh=mesh, in_specs=in_specs, out_specs=out_specs, check_vma=False
    )
```

```python
import functools
import math

import jax
import jax.numpy as jnp
import numpy as np
from jax import lax
from jax.experimental import pallas as pl
from jax.experimental.pallas import tpu as pltpu
from jax.sharding import PartitionSpec as P

F32 = jnp.float32
PITCH = 72
BF16 = jnp.bfloat16
VMEM = pltpu.VMEM
SMEM = pltpu.SMEM


def phase_angle_parts(points):
    index = jnp.arange(points, dtype=jnp.int32)
    windings = index[:, None] * index[None, :] % points
    angles = windings.astype(F32) * (2.0 * math.pi / points)
    return (jnp.cos(angles), jnp.sin(angles))


def row_table_of(points):
    cosine, sine_part = phase_angle_parts(points)
    upper_rows = jnp.concatenate([cosine, -sine_part], 1)
    lower_rows = jnp.concatenate([sine_part, cosine], 1)
    return jnp.concatenate([upper_rows, lower_rows], 0).astype(BF16)


def turn_orbitals(orb_ref, spread):
    norb = orb_ref.shape[0]
    pitch = spread.shape[0] // 32
    for g in range(norb // 4):
        turned = orb_ref[4 * g : 4 * g + 4].reshape(128, 128).astype(F32).T
        for o in range(4):
            lanes = [turned[32 * t : 32 * t + 32, 32 * o : 32 * o + 32] for t in range(4)]
            spread[pl.ds(4 * g + o, 32, stride=pitch), :] = jnp.concatenate(lanes, 1)
    rows = [spread[pitch * yp : pitch * yp + norb] for yp in range(32)]
    return jnp.concatenate(rows, 0).reshape(16, 2 * norb, 128)


def open_kernel(pairs_ref, vir_ref, occ_ref, out_ref, spread, spread_occ):
    out_ref[:, :64] = turn_orbitals(vir_ref, spread).astype(BF16)
    row = lax.broadcasted_iota(jnp.int32, (16, 8, 128), 1)
    told = jnp.where(row == 0, pairs_ref[0, 0], jnp.where(row == 1, pairs_ref[0, 1], 0))
    rest = [turn_orbitals(occ_ref, spread_occ), told.astype(F32)]
    out_ref[:, 64:] = jnp.concatenate(rest, 1).astype(BF16)


def open_up(pairs, virtual, occupied):
    return pl.pallas_call(
        open_kernel,
        out_shape=jax.ShapeDtypeStruct((16, 80, 128), BF16),
        in_specs=[pl.BlockSpec(memory_space=SMEM)] + [pl.BlockSpec(memory_space=VMEM)] * 2,
        out_specs=pl.BlockSpec(memory_space=VMEM),
        scratch_shapes=[pltpu.VMEM((32 * 40, 128), F32), pltpu.VMEM((32 * 8, 128), F32)],
        name="open_up",
    )(pairs, virtual, occupied)


def pick_kernel(got_ref, vir_ref, occ_ref):
    points = [got_ref[q, 64:].astype(F32).astype(jnp.int32) for q in range(16)]
    for q in range(16):
        vir_ref[q] = got_ref[points[q][9, 0], :64]
    for q in range(0, 16, 2):
        two = [got_ref[points[q + n][8, 0], 64:].astype(F32)[:8] for n in range(2)]
        occ_ref[q // 2] = jnp.concatenate(two, 0).astype(BF16)


def pick(got):
    return pl.pallas_call(
        pick_kernel,
        out_shape=[jax.ShapeDtypeStruct((16, 64, 128), BF16), jax.ShapeDtypeStruct((8, 16, 128), BF16)],
        in_specs=[pl.BlockSpec(memory_space=VMEM)],
        out_specs=[pl.BlockSpec(memory_space=VMEM)] * 2,
        name="pick",
    )(got)


CAME_BY = ((0, 4), (7, 3), (1, 5), (6, 2))


def deal_kernel(z_ref, *refs):
    got_refs, (out_ref, held) = refs[:4], refs[4:]
    for got_ref, steps in zip(got_refs, CAME_BY):
        for n in range(2):
            held[steps[n]] = got_ref[n].astype(F32)
    for g in range(2):
        for m in range(0, 4, 2):
            sources = [(4 * g + m + n - z_ref[0] + 8) % 8 for n in range(2)]
            for q in range(16):
                spot = 8 * (q % 2)
                rows = jnp.concatenate([held[s, q // 2, spot : spot + 8] for s in sources], 0)
                out_ref[2 * q + g, 8 * m : 8 * m + 16] = rows.astype(BF16)


def deal(z, got):
    return pl.pallas_call(
        deal_kernel,
        out_shape=jax.ShapeDtypeStruct((32, 32, 128), BF16),
        in_specs=[pl.BlockSpec(memory_space=SMEM)] + [pl.BlockSpec(memory_space=VMEM)] * 4,
        out_specs=pl.BlockSpec(memory_space=VMEM),
        scratch_shapes=[pltpu.VMEM((8, 8, 16, 128), F32)],
        name="deal",
    )(z, *got)


def weight_kernel(half_ref, column_ref, occ_ref, spread_ref, cos_ref, sin_ref, out_ref):
    half = half_ref[0]

    def step(yp, carry):
        piece, odd = yp // 2, yp % 2
        occ = jnp.concatenate([occ_ref[2 * piece + half], occ_ref[2 * piece + 1 - half]], 0)
        wide = lax.dot_general(occ, spread_ref[odd], (((0,), (0,)), ((), ())), preferred_element_type=F32)
        for g in range(2):
            ac, as_ = cos_ref[g], sin_ref[g]
            for u in range(2):
                c, s = column_ref[0, 32 * u + yp], column_ref[1, 32 * u + yp]
                tr = ac * c - as_ * s
                ti = as_ * c + ac * s
                real = wide[32 * u : 32 * u + 32, 128 * g : 128 * g + 128]
                imag = wide[64 + 32 * u : 96 + 32 * u, 128 * g : 128 * g + 128]
                wr = (real * tr + imag * ti).astype(BF16)
                wi = real * ti - imag * tr
                base = 128 * g + 32 * u
                out_ref[yp, base : base + 32, :128] = wr
                out_ref[yp, base : base + 32, 128:] = wi.astype(BF16)
                out_ref[yp, base + 64 : base + 96, :128] = (-wi).astype(BF16)
                out_ref[yp, base + 64 : base + 96, 128:] = wr
        return carry

    lax.fori_loop(0, 32, step, 0, unroll=8)


def weights_of(half, column, occ, spread, cosine, sine_part):
    return pl.pallas_call(
        weight_kernel,
        out_shape=jax.ShapeDtypeStruct((32, 256, 256), BF16),
        in_specs=[pl.BlockSpec(memory_space=SMEM)] * 2 + [pl.BlockSpec(memory_space=VMEM)] * 4,
        out_specs=pl.BlockSpec(memory_space=VMEM),
        compiler_params=pltpu.CompilerParams(vmem_limit_bytes=24 << 20),
        cost_estimate=pl.CostEstimate(flops=32 * 2 * 128 * 32 * 256, bytes_accessed=6 << 20, transcendentals=0),
        name="weights",
    )(half, column, occ, spread, cosine, sine_part)


def chunk_kernel(parts, place_ref, *refs):
    vir_refs, (weight_ref, row_ref, scale_ref, _, out_ref, total, ready, sems) = refs[:-8], refs[-8:]
    lane = lax.broadcasted_iota(jnp.int32, (32, 256), 1)
    upper = (lane // 32) % 2 == 0
    copies = []
    for n, part in enumerate(parts):
        here = vir_refs[: 2 * part]
        vir_refs = vir_refs[2 * part :]
        yp = 0
        for own_ref, other_ref in zip(here[0::2], here[1::2]):
            for step in range(own_ref.shape[0]):
                both = jnp.concatenate([own_ref[step], other_ref[step]], 1)
                nought = jnp.zeros_like(both)
                split = jnp.concatenate([jnp.where(upper, both, nought), jnp.where(upper, nought, both)], 0)
                sums = jnp.dot(split, weight_ref[yp], preferred_element_type=F32)
                for u in range(2):
                    for c in range(2):
                        block = sums[32 * u : 32 * u + 32, 128 * c : 128 * c + 128]
                        total[n, c, pl.ds(32 * u + yp, 32, stride=PITCH), :] = block
                yp += 1

        for a in range(32):
            left = jnp.concatenate([total[n, c, PITCH * a : PITCH * a + 64, :] for c in range(2)], 0).astype(BF16)
            result = lax.dot_general(left, row_ref[...], (((0,), (0,)), ((), ())), preferred_element_type=F32)
            ready[n, :, a] = (result.reshape(16, 8, 128) * scale_ref[...][None]).astype(BF16)
            if a % 8 == 7:
                copy = pltpu.make_async_copy(
                    ready.at[n, :, pl.ds(a - 7, 8)],
                    out_ref.at[:, pl.ds(32 * place_ref[n] + (a - 7), 8)],
                    sems.at[n, a // 8],
                )
                copy.start()
                copies.append(copy)
    for copy in copies:
        copy.wait()


def chunk(places, virs, weights, row_table, scale, out):
    n = len(virs)
    args = [v for vir in virs for v in vir] + [weights, row_table, scale]
    return pl.pallas_call(
        functools.partial(chunk_kernel, [len(vir) // 2 for vir in virs]),
        out_shape=jax.ShapeDtypeStruct(out.shape, BF16),
        in_specs=[pl.BlockSpec(memory_space=SMEM)]
        + [pl.BlockSpec(memory_space=VMEM)] * len(args)
        + [pl.BlockSpec(memory_space=pl.ANY)],
        out_specs=pl.BlockSpec(memory_space=pl.ANY),
        scratch_shapes=[
            pltpu.VMEM((n, 2, 32 * PITCH, 128), F32),
            pltpu.VMEM((n, 16, 32, 8, 128), BF16),
            pltpu.SemaphoreType.DMA((n, 4)),
        ],
        input_output_aliases={len(args) + 1: 0},
        compiler_params=pltpu.CompilerParams(vmem_limit_bytes=24 << 20),
        cost_estimate=pl.CostEstimate(flops=n << 31, bytes_accessed=n << 20, transcendentals=0),
        name="chunk",
    )(jnp.stack(places), *args, out)


def empty_kernel(out_ref):
    pass


def empty(shape):
    return pl.pallas_call(
        empty_kernel,
        out_shape=jax.ShapeDtypeStruct(shape, BF16),
        out_specs=pl.BlockSpec(memory_space=pl.ANY),
        name="empty",
    )()


def spread_table():
    table = np.zeros((2, 2, 4, 2, 4, 2, 16, 8), np.float32)
    for u in range(2):
        for g in range(2):
            for m in range(4):
                for o in range(4):
                    table[u, g, m, u, o, g, 4 * m + o, :] = 1.0
    return jnp.asarray(table.reshape(2, 64, 256), BF16)


def on_device(occupied, virtual, coulomb, transfer_pairs, shifts):
    points = 64
    z, half = lax.axis_index("kp"), lax.axis_index("ga")
    got = lax.all_to_all(open_up(transfer_pairs, virtual[0], occupied[0]), "ka", 0, 0, tiled=False)
    picked, occ = pick(got)
    own = lax.all_to_all(picked, "ka", 0, 0, tiled=False).reshape(32, 32, 128)
    two = jnp.stack([occ, lax.ppermute(occ, "kp", [(i, (i + 4) % 8) for i in range(8)])])
    occ = [two] + [lax.ppermute(two, "kp", [(i, (i + s) % 8) for i in range(8)]) for s in (1, -1, 2)]

    grid = jnp.arange(points, dtype=jnp.int32)
    cosine, sine_part = phase_angle_parts(points)
    planes = 8 * z + jnp.arange(8, dtype=jnp.int32)
    col_cos = jnp.take(cosine, planes, axis=0).astype(BF16).astype(F32).T
    col_sin = jnp.take(sine_part, planes, axis=0).astype(BF16).astype(F32).T
    turn_x = ((shifts[0, 0] * grid) % points).astype(F32) * (2.0 * math.pi / points)
    turn_y = ((shifts[0, 1] * grid) % points).astype(F32) * (2.0 * math.pi / points)
    cx, sx = jnp.cos(turn_x)[:, None], -jnp.sin(turn_x)[:, None]
    tab_cos = jnp.tile(col_cos * cx + col_sin * sx, (1, 16)).reshape(2, 32, 128)
    tab_sin = jnp.tile(col_cos * sx - col_sin * cx, (1, 16)).reshape(2, 32, 128)
    column = jnp.stack([jnp.cos(turn_y), -jnp.sin(turn_y)])
    scale = lax.dynamic_slice_in_dim(coulomb[0], 8 * z, 8, 0)
    scale = jnp.concatenate([scale, scale], 1) * (1.0 / points)
    row_table = row_table_of(points)

    forward = [(i, (i + 1) % 8) for i in range(8)]
    backward = [(i, (i - 1) % 8) for i in range(8)]
    tab_cos = jnp.where(half == 0, tab_cos, tab_cos[::-1])
    tab_sin = jnp.where(half == 0, tab_sin, tab_sin[::-1])

    other = lax.ppermute(own, "ga", [(0, 1), (1, 0)])
    rounds = [([own, other],) * 2]
    for s in range(3):
        ahead = [lax.ppermute(v, "kp", forward) for v in rounds[s][0]]
        behind = [lax.ppermute(v, "kp", backward) for v in rounds[s][1]]
        rounds.append((ahead, behind))
    occ = lax.optimization_barrier((rounds[1][0][0], *occ))[1:]
    occ = lax.all_to_all(deal(z.reshape(1), occ), ("ka", "ga"), 0, 0, tiled=False)
    weights = weights_of(half.reshape(1), column, occ, spread_table(), tab_cos, tab_sin)

    def add(shifted, virs, out):
        return chunk([(z - s) % 8 for s in shifted], virs, weights, row_table, scale, out)

    out = add([0], [rounds[0][0]], empty((16, 256, 8, 128)))
    for s in range(1, 4):
        out = add([s, -s], rounds[s], out)
    lower = [lax.ppermute(v[:16], "kp", forward) for v in ahead]
    higher = [lax.ppermute(v[16:], "kp", backward) for v in behind]
    out = add([4], [lower + higher], out)
    return out[None]


def solution(mesh):
    in_specs = (
        P("ka", "kp", "ga", None),
        P("ka", "kp", "ga", None),
        P("ka", None, None),
        P("ka", None),
        P("ka", None),
    )
    out_specs = P("ka", "ga", None, "kp", None)
    return jax.shard_map(
        on_device, mesh=mesh, in_specs=in_specs, out_specs=out_specs, check_vma=False
    )
```
